32 devices in a mesh: req: 8 (over z, x), kv: 4 (over y, core).
Axes of the slice: x: 2, y: 2, z: 4, core: 2. Of those that a mesh axis runs over, the one named last changes fastest.
Arguments:
- residual_in: bfloat16 [256, 4096], P(None, 'req'), may hold values from -6 to 6
- attn_gain: float32 [4096], replicated, may hold values from 0.1 to 1.9
- query_weight: bfloat16 [4096, 4096], P(None, 'kv'), may hold values from -0.09375 to 0.09375
- key_matrix: bfloat16 [4096, 1024], P(None, 'kv'), may hold values from -0.09375 to 0.09375
- value_matrix: bfloat16 [4096, 1024], P(None, 'kv'), may hold values from -0.09375 to 0.09375
- key_cache: bfloat16 [256, 8, 640, 128], P('req', 'kv'), may hold values from -400 to 400
- cached_values: bfloat16 [256, 8, 640, 128], P('req', 'kv'), may hold values from -6 to 6
- cache_lengths: int32 [256], P('req'), may hold values from 1 to 640, as said below
- positions: int32 [256], P('req'), may hold values from 640 to 16383
- output_weight: bfloat16 [4096, 4096], P(None, 'req'), may hold values from -0.09375 to 0.09375
- mlp_gain: float32 [4096], P('req'), may hold values from 0.1 to 1.9
- gate_weight: bfloat16 [4096, 14336], P('req', 'kv'), may hold values from -0.09375 to 0.09375
- up_weight: bfloat16 [4096, 14336], P('req', 'kv'), may hold values from -0.09375 to 0.09375
- down_weight: bfloat16 [14336, 4096], P('kv', 'req'), may hold values from -0.046875 to 0.046875
Outputs:
- output: bfloat16 [256, 4096], P('kv', 'req')
The draws below stay inside these ranges and needn't reach their ends.
Inputs may be any that keep to these rules, and one draw needn't show every extreme that they name: `cache_lengths`: each request's filled slots; some request has exactly 640 and some exactly 1.
All inputs are finite; a program needn't handle non-finite values.
Results may differ from the reference program's by a relative error of at most 0.025.
Values may be sent and summed in bfloat16 or wider, within the bound.
No kernel may reach another device: no remote copies, remote signals or barrier semaphores. Data moves between devices by JAX's collectives and lax.ppermute only.
A program may use at most 128 MiB of HBM per device.

```python
import math
import jax
import jax.numpy as jnp
from jax import lax

MODEL_WIDTH = 4096
FF = 14336
QUERY_HEADS = 32
KEY_VALUE_HEADS = 8
HEAD_WIDTH = 128
CACHE_LENGTH = 640
WINDOW = 512
SINKS = 4
REQ_DEV = 32
REQUEST_TOTAL = 256


def draw_key_cache(key, part):
    array_shape = (REQUEST_TOTAL, KEY_VALUE_HEADS, CACHE_LENGTH, HEAD_WIDTH)
    return jnp.clip(jax.random.normal(key, array_shape, jnp.float32), -6.0, 6.0).astype(jnp.bfloat16)


def draw_cache_lengths(key, part):
    first, second = jax.random.split(jax.random.fold_in(key, 7))
    groups = REQUEST_TOTAL // REQ_DEV
    factor = jax.random.randint(first, (groups,), 1, 5)
    factor = jnp.repeat(factor, REQ_DEV)
    base = jax.random.randint(second, (REQUEST_TOTAL,), 0, CACHE_LENGTH)
    filled = 1 + base * factor // 4
    filled = filled.at[0].set(CACHE_LENGTH)
    filled = filled.at[1].set(1)
    return filled.astype(jnp.int32)


def place_ends(result, key, least, largest):
    place = [jax.random.randint(jax.random.fold_in(key, axis), (), 0, length) for axis, length in enumerate(result.shape)]
    widest = result.shape.index(max(result.shape))
    beside = place[:widest] + [(place[widest] + 1) % result.shape[widest]] + place[widest + 1:]
    return result.at[tuple(place)].set(least).at[tuple(beside)].set(largest)


def steps_of(key, shape, pieces, low, high):
    loudness = 1.0
    for dim, shards_of in pieces:
        steps = jax.random.uniform(jax.random.fold_in(jax.random.fold_in(key, 6), dim), (shards_of,), jnp.float32, low / len(pieces), high / len(pieces))
        loudness = loudness * jnp.repeat(jnp.exp(steps), shape[dim] // shards_of).reshape((-1,) + (1,) * (len(shape) - 1 - dim))
    return loudness


def scatter_about(key, shape, deviation, most, pieces=(), kind=jnp.bfloat16):
    entries = deviation * jax.random.normal(key, shape, jnp.float32)
    if pieces:
        entries = entries * steps_of(key, shape, pieces, -0.22, 0.18)
    return jnp.clip(entries, -most, most).astype(kind)


def setup_inputs(seed: int = 0) -> dict:
    seeds = jax.random.split(jax.random.key(seed), 15)
    residual_in = scatter_about(seeds[0], (REQUEST_TOTAL, MODEL_WIDTH), 1.0, 6.0, ((1, 8),))
    attn_gain = jnp.clip(1.0 + 0.18 * jax.random.normal(seeds[1], (MODEL_WIDTH,), jnp.float32), 0.1, 1.9)
    query_weight = scatter_about(seeds[2], (MODEL_WIDTH, QUERY_HEADS * HEAD_WIDTH), MODEL_WIDTH ** -0.5, 0.09375, ((1, 4),))
    key_matrix = scatter_about(seeds[3], (MODEL_WIDTH, KEY_VALUE_HEADS * HEAD_WIDTH), MODEL_WIDTH ** -0.5, 0.09375, ((1, 4),))
    value_matrix = scatter_about(seeds[4], (MODEL_WIDTH, KEY_VALUE_HEADS * HEAD_WIDTH), MODEL_WIDTH ** -0.5, 0.09375, ((1, 4),))
    key_cache = draw_key_cache(jax.random.fold_in(seeds[14], 71), 0)
    cached_values = scatter_about(seeds[6], (REQUEST_TOTAL, KEY_VALUE_HEADS, CACHE_LENGTH, HEAD_WIDTH), 1.0, 6.0, ((0, 8), (1, 4)))
    cache_lengths = draw_cache_lengths(jax.random.fold_in(seeds[14], 71), 0)
    positions = place_ends(jax.random.randint(seeds[8], (REQUEST_TOTAL,), CACHE_LENGTH, 16384), jax.random.fold_in(seeds[8], 1), CACHE_LENGTH, 16383).astype(jnp.int32)
    output_weight = scatter_about(seeds[9], (QUERY_HEADS * HEAD_WIDTH, MODEL_WIDTH), (QUERY_HEADS * HEAD_WIDTH) ** -0.5, 0.09375, ((1, 8),))
    mlp_gain = jnp.clip(1.0 + 0.18 * jax.random.normal(seeds[10], (MODEL_WIDTH,), jnp.float32), 0.1, 1.9)
    gate_weight = scatter_about(seeds[11], (MODEL_WIDTH, FF), MODEL_WIDTH ** -0.5, 0.09375, ((0, 8), (1, 4)))
    up_weight = scatter_about(seeds[12], (MODEL_WIDTH, FF), MODEL_WIDTH ** -0.5, 0.09375, ((0, 8), (1, 4)))
    down_weight = scatter_about(seeds[13], (FF, MODEL_WIDTH), FF ** -0.5, 0.046875, ((0, 4), (1, 8)))
    return {"residual_in": residual_in, "attn_gain": attn_gain, "query_weight": query_weight, "key_matrix": key_matrix, "value_matrix": value_matrix, "key_cache": key_cache, "cached_values": cached_values, "cache_lengths": cache_lengths, "positions": positions, "output_weight": output_weight, "mlp_gain": mlp_gain, "gate_weight": gate_weight, "up_weight": up_weight, "down_weight": down_weight}


EPS = 1e-05
THETA = 10000.0

def apply_rotary(vectors, places):
    half = vectors.shape[-1] // 2
    freqs = jnp.exp(jnp.arange(half, dtype=jnp.float32) * (-2.0 * math.log(THETA) / vectors.shape[-1]))
    angles = places.astype(jnp.float32)[:, None] * freqs[None, :]
    cosine = jnp.cos(angles)[:, None, :]
    sine = jnp.sin(angles)[:, None, :]
    first = vectors[..., :half]
    second = vectors[..., half:]
    return jnp.concatenate([first * cosine - second * sine, second * cosine + first * sine], axis=-1)

def attend(query_rows, keys, values, new_key, new_value, allowed):
    factor = 1.0 / math.sqrt(query_rows.shape[-1])
    scores = jnp.einsum('bgd,bjd->bgj', query_rows.astype(jnp.float32), keys.astype(jnp.float32)) * factor
    scores = jnp.where(allowed[:, None, :], scores, -1e+30)
    own = jnp.einsum('bgd,bd->bg', query_rows.astype(jnp.float32), new_key.astype(jnp.float32)) * factor
    peak = jnp.maximum(lax.optimization_barrier(jnp.max(scores, axis=-1)), own)
    expo = jnp.where(allowed[:, None, :], jnp.exp(scores - peak[..., None]), 0.0)
    own_expo = jnp.exp(own - peak)
    denom = lax.optimization_barrier(jnp.sum(expo, axis=-1)) + own_expo
    weights = (expo / denom[..., None]).astype(jnp.bfloat16)
    own_weight = (own_expo / denom).astype(jnp.bfloat16)
    mixed = jnp.einsum('bgj,bjd->bgd', weights.astype(jnp.float32), values.astype(jnp.float32))
    mixed = mixed + own_weight.astype(jnp.float32)[..., None] * new_value.astype(jnp.float32)[:, None, :]
    return mixed.astype(jnp.bfloat16)

def reference(residual_in, attn_gain, query_weight, key_matrix, value_matrix, key_cache, cached_values, cache_lengths, positions, output_weight, mlp_gain, gate_weight, up_weight, down_weight):
    slot_count = residual_in.shape[0]
    query_group = QUERY_HEADS // KEY_VALUE_HEADS
    stream = residual_in.astype(jnp.float32)
    normed_input = (stream / jnp.sqrt(lax.optimization_barrier(jnp.sum(stream * stream, axis=-1, keepdims=True)) / MODEL_WIDTH + EPS) * attn_gain).astype(jnp.bfloat16)
    query_rows = jnp.dot(normed_input, query_weight, preferred_element_type=jnp.float32).reshape(slot_count, QUERY_HEADS, HEAD_WIDTH)
    query_rows = apply_rotary(query_rows, positions).astype(jnp.bfloat16).reshape(slot_count, KEY_VALUE_HEADS, query_group, HEAD_WIDTH)
    fresh_keys = jnp.dot(normed_input, key_matrix, preferred_element_type=jnp.float32).reshape(slot_count, KEY_VALUE_HEADS, HEAD_WIDTH)
    fresh_keys = apply_rotary(fresh_keys, positions).astype(jnp.bfloat16)
    fresh_values = jnp.dot(normed_input, value_matrix, preferred_element_type=jnp.float32).reshape(slot_count, KEY_VALUE_HEADS, HEAD_WIDTH).astype(jnp.bfloat16)
    slots = jnp.arange(CACHE_LENGTH, dtype=jnp.int32)[None, :]
    limit = cache_lengths[:, None]
    allowed = (slots < limit) & ((slots < SINKS) | (slots > limit - WINDOW))

    def per_head_rows(head):
        keys = lax.dynamic_index_in_dim(key_cache, head, 1, keepdims=False)
        values = lax.dynamic_index_in_dim(cached_values, head, 1, keepdims=False)
        heads_q = lax.dynamic_index_in_dim(query_rows, head, 1, keepdims=False)
        own_key = lax.dynamic_index_in_dim(fresh_keys, head, 1, keepdims=False)
        own_value = lax.dynamic_index_in_dim(fresh_values, head, 1, keepdims=False)
        return attend(heads_q, keys, values, own_key, own_value, allowed)
    attended_rows = lax.map(per_head_rows, jnp.arange(KEY_VALUE_HEADS, dtype=jnp.int32))
    attended_rows = jnp.transpose(attended_rows, (1, 0, 2, 3)).reshape(slot_count, QUERY_HEADS * HEAD_WIDTH)
    middle = stream + jnp.dot(attended_rows, output_weight, preferred_element_type=jnp.float32)
    scaled = (middle * mlp_gain).astype(jnp.bfloat16)
    inverse = 1.0 / jnp.sqrt(lax.optimization_barrier(jnp.sum(middle * middle, axis=-1, keepdims=True)) / MODEL_WIDTH + EPS)
    gate = jnp.dot(scaled, gate_weight, preferred_element_type=jnp.float32) * inverse
    upper = jnp.dot(scaled, up_weight, preferred_element_type=jnp.float32) * inverse
    hidden = (jax.nn.silu(gate) * upper).astype(jnp.bfloat16)
    return (middle + jnp.dot(hidden, down_weight, preferred_element_type=jnp.float32)).astype(jnp.bfloat16)
```

```python
import math

import jax
import jax.numpy as jnp
from jax import lax
from jax.sharding import PartitionSpec as P

MODEL_WIDTH = 4096
WINDOW = 512
SINKS = 4


EPS = 1e-05
THETA = 10000.0


def rotary_tables(places, head_size):
    half = head_size // 2
    freqs = jnp.exp(jnp.arange(half, dtype=jnp.float32) * (-2.0 * math.log(THETA) / head_size))
    angles = places.astype(jnp.float32)[:, None] * freqs[None, :]
    return jnp.cos(angles), jnp.sin(angles)


def rotate(flat, cosine, sine, head_size):
    half = head_size // 2
    heads = []
    for start in range(0, flat.shape[1], head_size):
        first = flat[:, start : start + half]
        second = flat[:, start + half : start + head_size]
        heads.append(first * cosine - second * sine)
        heads.append(second * cosine + first * sine)
    return jnp.concatenate(heads, axis=1).astype(jnp.bfloat16)


def attend(query_rows, keys, values, new_key, new_value, allowed):
    factor = 1.0 / math.sqrt(query_rows.shape[-1])
    scores = (
        jnp.einsum("bgd,bjd->bgj", query_rows, keys, preferred_element_type=jnp.float32) * factor
    )
    scores = jnp.where(allowed[:, None, :], scores, -1e30)
    own = jnp.einsum("bgd,bd->bg", query_rows, new_key, preferred_element_type=jnp.float32) * factor
    peak = jnp.maximum(jnp.max(scores, axis=-1), own)
    expo = jnp.where(allowed[:, None, :], jnp.exp(scores - peak[..., None]), 0.0)
    own_expo = jnp.exp(own - peak)
    denom = jnp.sum(expo, axis=-1) + own_expo
    weights = (expo / denom[..., None]).astype(jnp.bfloat16)
    own_weight = (own_expo / denom).astype(jnp.bfloat16)
    mixed = jnp.einsum("bgj,bjd->bgd", weights, values, preferred_element_type=jnp.float32)
    mixed = (
        mixed
        + own_weight.astype(jnp.float32)[..., None] * new_value.astype(jnp.float32)[:, None, :]
    )
    return mixed.astype(jnp.bfloat16)


def bit_reverse(value, bits):
    result = 0
    for bit in range(bits):
        result |= ((value >> bit) & 1) << (bits - 1 - bit)
    return result


def exchange(value, size, bit):
    return lax.ppermute(value, "req", [(i, i ^ (1 << bit)) for i in range(size)])


def local_order(value, place, size):
    bits = size.bit_length() - 1
    rows = value.shape[0] // size
    return jnp.concatenate(
        [
            lax.dynamic_slice_in_dim(value, (place ^ bit_reverse(i, bits)) * rows, rows, 0)
            for i in range(size)
        ],
        axis=0,
    )


def natural_order(value, place, size):
    bits = size.bit_length() - 1
    rows = value.shape[0] // size
    pieces = []
    for block in range(size):
        other = place ^ block
        spot = jnp.int32(0)
        for bit in range(bits):
            spot = spot | (((other >> bit) & 1) << (bits - 1 - bit))
        pieces.append(lax.dynamic_slice_in_dim(value, spot * rows, rows, 0))
    return jnp.concatenate(pieces, axis=0)


def gather_rows(value, size):
    for bit in reversed(range(size.bit_length() - 1)):
        value = jnp.concatenate([value, exchange(value, size, bit)], axis=0)
    return value


def scatter_sum(value, size):
    for bit in range(size.bit_length() - 1):
        half = value.shape[0] // 2
        other = exchange(value[half:], size, bit)
        value = (value[:half].astype(jnp.float32) + other.astype(jnp.float32)).astype(jnp.bfloat16)
    return value


def chunks_of(columns):
    tiles = columns // 128
    for count in (4, 2, 1):
        if tiles % count == 0:
            return count
    return 1


def shards(
    residual_in,
    attn_gain,
    query_weight,
    key_matrix,
    value_matrix,
    key_cache,
    cached_values,
    cache_lengths,
    positions,
    output_weight,
    mlp_gain,
    gate_weight,
    up_weight,
    down_weight,
):
    req_size = lax.axis_size("req")
    kv_size = lax.axis_size("kv")
    req_place = lax.axis_index("req")
    kv_place = lax.axis_index("kv")
    tokens = lax.all_to_all(residual_in, "req", split_axis=0, concat_axis=1, tiled=True)
    local_rows = tokens.shape[0]
    heads_here = key_cache.shape[1]
    head_size = key_cache.shape[3]
    query_group = query_weight.shape[1] // (heads_here * head_size)
    stream = tokens.astype(jnp.float32)
    normed_input = (
        stream
        / jnp.sqrt(jnp.sum(stream * stream, axis=-1, keepdims=True) / MODEL_WIDTH + EPS)
        * attn_gain
    ).astype(jnp.bfloat16)
    cosine, sine = rotary_tables(positions, head_size)
    query_rows, fresh_keys, fresh_values = lax.optimization_barrier(
        (
            jnp.dot(normed_input, query_weight, preferred_element_type=jnp.float32),
            jnp.dot(normed_input, key_matrix, preferred_element_type=jnp.float32),
            jnp.dot(normed_input, value_matrix, preferred_element_type=jnp.float32),
        )
    )
    query_rows = rotate(query_rows, cosine, sine, head_size).reshape(
        local_rows, heads_here, query_group, head_size
    )
    fresh_keys = rotate(fresh_keys, cosine, sine, head_size).reshape(
        local_rows, heads_here, head_size
    )
    fresh_values = fresh_values.astype(jnp.bfloat16).reshape(local_rows, heads_here, head_size)
    slots = jnp.arange(key_cache.shape[2], dtype=jnp.int32)[None, :]
    limit = cache_lengths[:, None]
    allowed = (slots < limit) & ((slots < SINKS) | (slots > limit - WINDOW))
    results = []
    for head in range(heads_here):
        results.append(
            attend(
                query_rows[:, head],
                key_cache[:, head],
                cached_values[:, head],
                fresh_keys[:, head],
                fresh_values[:, head],
                allowed,
            )
        )
    attended_rows = jnp.stack(results, axis=1).reshape(
        local_rows, heads_here * query_group * head_size
    )
    features = attended_rows.shape[1]
    weight_rows = lax.dynamic_slice_in_dim(output_weight, kv_place * features, features, 0)
    residual_rows = local_order(residual_in, req_place, req_size).astype(jnp.float32)
    partial_mix = jnp.dot(
        gather_rows(attended_rows, req_size),
        weight_rows,
        preferred_element_type=jnp.float32,
    ).astype(jnp.bfloat16)
    total_rows = partial_mix.shape[0]
    pieces = lax.all_to_all(
        partial_mix.reshape(kv_size, total_rows // kv_size, -1), "kv", split_axis=0, concat_axis=0
    )
    mixed_share = jnp.sum(pieces.astype(jnp.float32), axis=0).astype(jnp.bfloat16)
    mixed = lax.all_gather(mixed_share, "kv", axis=0, tiled=True)
    middle = residual_rows + mixed.astype(jnp.float32)
    scaled = (middle * mlp_gain).astype(jnp.bfloat16)
    squares = jnp.sum(middle * middle, axis=-1, keepdims=True)
    count = chunks_of(gate_weight.shape[1])
    width = gate_weight.shape[1] // count
    inverse = None
    partial_out = None
    sums = []
    for chunk in range(count):
        columns = slice(chunk * width, (chunk + 1) * width)
        parts = [
            jnp.dot(scaled, gate_weight[:, columns], preferred_element_type=jnp.float32),
            jnp.dot(scaled, up_weight[:, columns], preferred_element_type=jnp.float32),
        ]
        if chunk == 0:
            parts.append(jnp.broadcast_to(squares, (total_rows, 128)))
        sums.append(scatter_sum(jnp.concatenate(parts, axis=1).astype(jnp.bfloat16), req_size))
    for chunk in range(count):
        total = sums[chunk].astype(jnp.float32)
        if chunk == 0:
            inverse = 1.0 / jnp.sqrt(total[:, 2 * width : 2 * width + 1] / MODEL_WIDTH + EPS)
        hidden = (
            jax.nn.silu(total[:, :width] * inverse) * (total[:, width : 2 * width] * inverse)
        ).astype(jnp.bfloat16)
        product = jnp.dot(
            gather_rows(hidden, req_size),
            down_weight[chunk * width : (chunk + 1) * width],
            preferred_element_type=jnp.float32,
        )
        partial_out = product if partial_out is None else partial_out + product
    ordered = natural_order(partial_out.astype(jnp.bfloat16), req_place, req_size)
    pieces = lax.all_to_all(
        ordered.reshape(kv_size, total_rows // kv_size, -1), "kv", split_axis=0, concat_axis=0
    )
    share = total_rows // kv_size
    base_rows = lax.dynamic_slice_in_dim(
        natural_order(middle, req_place, req_size), kv_place * share, share, 0
    )
    return (base_rows + jnp.sum(pieces.astype(jnp.float32), axis=0)).astype(jnp.bfloat16)


def solution(mesh):
    return jax.shard_map(
        shards,
        mesh=mesh,
        in_specs=(
            P(None, "req"),
            P(),
            P(None, "kv"),
            P(None, "kv"),
            P(None, "kv"),
            P("req", "kv", None, None),
            P("req", "kv", None, None),
            P("req"),
            P("req"),
            P(None, "req"),
            P("req"),
            P("req", "kv"),
            P("req", "kv"),
            P("kv", "req"),
        ),
        out_specs=P("kv", "req"),
        check_vma=False,
    )
```

```python
import math

import jax
import jax.numpy as jnp
from jax import lax
from jax.experimental import pallas as pl
from jax.experimental.pallas import tpu as pltpu
from jax.sharding import PartitionSpec as P

MODEL_WIDTH = 4096
WINDOW = 512
SINKS = 4


EPS = 1e-05
THETA = 10000.0


def rotary_tables(places, head_size):
    half = head_size // 2
    freqs = jnp.exp(jnp.arange(half, dtype=jnp.float32) * (-2.0 * math.log(THETA) / head_size))
    angles = places.astype(jnp.float32)[:, None] * freqs[None, :]
    return jnp.cos(angles), jnp.sin(angles)


def rotate(flat, cosine, sine, head_size):
    half = head_size // 2
    heads = []
    for start in range(0, flat.shape[1], head_size):
        first = flat[:, start : start + half]
        second = flat[:, start + half : start + head_size]
        heads.append(first * cosine - second * sine)
        heads.append(second * cosine + first * sine)
    return jnp.concatenate(heads, axis=1).astype(jnp.bfloat16)


def attend(query_rows, keys, values, new_key, new_value, allowed):
    factor = 1.0 / math.sqrt(query_rows.shape[-1])
    scores = (
        jnp.einsum("bgd,bjd->bgj", query_rows, keys, preferred_element_type=jnp.float32) * factor
    )
    scores = jnp.where(allowed[:, None, :], scores, -1e30)
    own = jnp.einsum("bgd,bd->bg", query_rows, new_key, preferred_element_type=jnp.float32) * factor
    peak = jnp.maximum(jnp.max(scores, axis=-1), own)
    expo = jnp.where(allowed[:, None, :], jnp.exp(scores - peak[..., None]), 0.0)
    own_expo = jnp.exp(own - peak)
    denom = jnp.sum(expo, axis=-1) + own_expo
    weights = (expo / denom[..., None]).astype(jnp.bfloat16)
    own_weight = (own_expo / denom).astype(jnp.bfloat16)
    mixed = jnp.einsum("bgj,bjd->bgd", weights, values, preferred_element_type=jnp.float32)
    mixed = (
        mixed
        + own_weight.astype(jnp.float32)[..., None] * new_value.astype(jnp.float32)[:, None, :]
    )
    return mixed.astype(jnp.bfloat16)


def bit_reverse(value, bits):
    result = 0
    for bit in range(bits):
        result |= ((value >> bit) & 1) << (bits - 1 - bit)
    return result


def exchange(value, size, bit):
    return lax.ppermute(value, "req", [(i, i ^ (1 << bit)) for i in range(size)])


def local_order(value, place, size):
    bits = size.bit_length() - 1
    rows = value.shape[0] // size
    return jnp.concatenate(
        [
            lax.dynamic_slice_in_dim(value, (place ^ bit_reverse(i, bits)) * rows, rows, 0)
            for i in range(size)
        ],
        axis=0,
    )


def local_spot(place, block, size):
    bits = size.bit_length() - 1
    other = place ^ block
    spot = jnp.int32(0)
    for bit in range(bits):
        spot = spot | (((other >> bit) & 1) << (bits - 1 - bit))
    return spot


def gather_rows(value, size):
    for bit in reversed(range(size.bit_length() - 1)):
        value = jnp.concatenate([value, exchange(value, size, bit)], axis=0)
    return value


def kv_exchange(value, size, bit):
    return lax.ppermute(value, "kv", [(i, i ^ (1 << bit)) for i in range(size)])


def kv_sum(value, place, size):
    half = value.shape[0] // 2
    mine = lax.rem(place, 2)
    pair = value.astype(jnp.float32) + kv_exchange(value, size, 0).astype(jnp.float32)
    part = lax.dynamic_slice_in_dim(pair, mine * half, half, 0)
    for bit in range(1, size.bit_length() - 1):
        part = part + kv_exchange(part.astype(jnp.bfloat16), size, bit).astype(jnp.float32)
    part = part.astype(jnp.bfloat16)
    other = kv_exchange(part, size, 0)
    return jnp.where(
        mine == 0, jnp.concatenate([part, other], axis=0), jnp.concatenate([other, part], axis=0)
    )


def chunks_of(columns):
    tiles = columns // 128
    for count in (4, 2, 1):
        if tiles % count == 0:
            return count
    return 1


class Chain:
    def __init__(self, token):
        self.token = token

    def run(self, body, outs, ins, in_specs=None, flops=0):
        specs = list(in_specs or [None] * len(ins))
        specs = [
            pl.BlockSpec(memory_space=pltpu.VMEM) if spec is None else spec for spec in specs
        ]
        count = len(ins)

        def kernel(*refs):
            body(*refs[:count], *refs[count + 1 :])

        results = pl.pallas_call(
            kernel,
            out_shape=outs,
            grid=(1,),
            in_specs=[*specs, pl.BlockSpec(memory_space=pl.ANY)],
            out_specs=[pl.BlockSpec(memory_space=pltpu.VMEM)] * len(outs),
            compiler_params=pltpu.CompilerParams(vmem_limit_bytes=32 * 1024 * 1024),
            cost_estimate=pl.CostEstimate(flops=0, bytes_accessed=0, transcendentals=0),
        )(*ins, self.token)
        self.token = results[0]
        return results


def array(shape, dtype):
    return jax.ShapeDtypeStruct(shape, dtype)


def project(chain, scaled, squares, gate, up, chunk, width):
    rows, depth = scaled.shape
    half = rows // 2
    total = 2 * width + (128 if squares is not None else 0)

    def body(scaled_ref, gate_ref, up_ref, *refs):
        send_ref, keep_ref = refs[-2:]
        for start, out_ref in ((half, send_ref), (0, keep_ref)):
            left = scaled_ref[start : start + half]
            out_ref[:, :width] = jnp.dot(
                left, gate_ref[...], preferred_element_type=jnp.float32
            ).astype(jnp.bfloat16)
            out_ref[:, width : 2 * width] = jnp.dot(
                left, up_ref[...], preferred_element_type=jnp.float32
            ).astype(jnp.bfloat16)
            if squares is not None:
                out_ref[:, 2 * width :] = jnp.broadcast_to(
                    refs[0][start : start + half], (half, 128)
                ).astype(jnp.bfloat16)

    ins, specs = [scaled, gate, up], [None]
    specs += [pl.BlockSpec((depth, width), lambda i: (0, chunk))] * 2
    if squares is not None:
        ins.append(squares)
        specs.append(None)
    out = array((half, total), jnp.bfloat16)
    return chain.run(body, [out, out], ins, specs, flops=4 * rows * depth * width)


def add_halve(chain, other, kept):
    half = kept.shape[0] // 2

    def body(other_ref, kept_ref, send_ref, keep_ref):
        for start, out_ref in ((half, send_ref), (0, keep_ref)):
            rows = slice(start, start + half)
            out_ref[...] = (
                other_ref[rows].astype(jnp.float32) + kept_ref[rows].astype(jnp.float32)
            ).astype(jnp.bfloat16)

    out = array((half, kept.shape[1]), jnp.bfloat16)
    return chain.run(body, [out, out], [other, kept])


def activate(chain, other, kept, inverse, width):
    rows = kept.shape[0]
    first = inverse is None

    def body(other_ref, kept_ref, *refs):
        def total(columns):
            return other_ref[:, columns].astype(jnp.float32) + kept_ref[:, columns].astype(
                jnp.float32
            )

        if first:
            hidden_ref, inverse_ref = refs
            scale = 1.0 / jnp.sqrt(total(slice(2 * width, 2 * width + 128)) / MODEL_WIDTH + EPS)
            inverse_ref[...] = scale
        else:
            scale_ref, hidden_ref = refs
            scale = scale_ref[...]
        scale = scale[:, :1]
        gate = total(slice(0, width)) * scale
        up = total(slice(width, 2 * width)) * scale
        hidden_ref[...] = (gate / (1.0 + jnp.exp(-gate)) * up).astype(jnp.bfloat16)

    outs = [array((rows, width), jnp.bfloat16)]
    ins = [other, kept]
    if first:
        outs.append(array((rows, 128), jnp.float32))
    else:
        ins.append(inverse)
    results = chain.run(body, outs, ins)
    return results if first else (results[0], inverse)


def join(chain, kept, other):
    rows = kept.shape[0]

    def body(kept_ref, other_ref, out_ref):
        out_ref[:rows] = kept_ref[...]
        out_ref[rows:] = other_ref[...]

    return chain.run(body, [array((2 * rows, kept.shape[1]), kept.dtype)], [kept, other])[0]


def lower(chain, kept, other, down, chunk, width, carried):
    half = kept.shape[0]
    columns = down.shape[1]

    def body(kept_ref, other_ref, down_ref, *refs):
        out_ref = refs[-1]
        for start, hidden_ref in ((0, kept_ref), (half, other_ref)):
            rows = slice(start, start + half)
            product = jnp.dot(
                hidden_ref[...], down_ref[...], preferred_element_type=jnp.float32
            )
            out_ref[rows] = product if carried is None else refs[0][rows] + product

    ins = [kept, other, down]
    specs = [None, None, pl.BlockSpec((width, columns), lambda i: (chunk, 0))]
    if carried is not None:
        ins.append(carried)
        specs.append(None)
    return chain.run(
        body,
        [array((2 * half, columns), jnp.float32)],
        ins,
        specs,
        flops=4 * half * width * columns,
    )[0]


def split_for_kv(chain, total, places, req_size, kv_size):
    rows, columns = total.shape
    bits = req_size.bit_length() - 1
    block = rows // req_size
    per = req_size // kv_size

    def body(places_ref, total_ref, send_ref, keep_ref):
        req_place, mine = places_ref[0], places_ref[1]
        for spot in range(req_size):
            actual = req_place ^ bit_reverse(spot, bits)
            owner = actual // per
            start = pl.multiple_of(((owner // 2) * per + actual % per) * block, block)
            value = total_ref[spot * block : (spot + 1) * block].astype(jnp.bfloat16)

            @pl.when(owner % 2 == mine)
            def _():
                keep_ref[pl.ds(start, block)] = value

            @pl.when(owner % 2 != mine)
            def _():
                send_ref[pl.ds(start, block)] = value

    out = array((rows // 2, columns), jnp.bfloat16)
    return chain.run(
        body,
        [out, out],
        [places, total],
        [pl.BlockSpec(memory_space=pltpu.SMEM), None],
    )


def feed_forward(scaled, squares, gate_weight, up_weight, down_weight, req_size):
    bits = req_size.bit_length() - 1
    count = chunks_of(gate_weight.shape[1])
    width = gate_weight.shape[1] // count
    chain = Chain(scaled)
    kept, moving = {}, {}
    state = {"inverse": None, "total": None}

    def step(chunk, stage):
        if stage == 0:
            send, kept[chunk] = project(
                chain, scaled, squares if chunk == 0 else None, gate_weight, up_weight, chunk, width
            )
            moving[chunk] = exchange(send, req_size, 0)
        elif stage < bits:
            send, kept[chunk] = add_halve(chain, moving[chunk], kept[chunk])
            moving[chunk] = exchange(send, req_size, stage)
        elif stage == bits:
            kept[chunk], state["inverse"] = activate(
                chain, moving[chunk], kept[chunk], state["inverse"], width
            )
            moving[chunk] = exchange(kept[chunk], req_size, bits - 1)
        elif stage < 2 * bits:
            kept[chunk] = join(chain, kept[chunk], moving[chunk])
            moving[chunk] = exchange(kept[chunk], req_size, 2 * bits - 1 - stage)
        else:
            state["total"] = lower(
                chain, kept[chunk], moving[chunk], down_weight, chunk, width, state["total"]
            )

    for chunk, stage in task_order(count, bits):
        step(chunk, stage)
    return chain, state["total"]


def task_order(count, bits):
    tasks = [(chunk, 0) for chunk in range(count)]
    for slot in range(1, count + 2 * bits):
        for chunk in range(count):
            if 1 <= slot - chunk <= 2 * bits:
                tasks.append((chunk, slot - chunk))
    return tasks


def shards(
    residual_in,
    attn_gain,
    query_weight,
    key_matrix,
    value_matrix,
    key_cache,
    cached_values,
    cache_lengths,
    positions,
    output_weight,
    mlp_gain,
    gate_weight,
    up_weight,
    down_weight,
):
    req_size = lax.axis_size("req")
    kv_size = lax.axis_size("kv")
    req_place = lax.axis_index("req")
    kv_place = lax.axis_index("kv")
    tokens = lax.all_to_all(residual_in, "req", split_axis=0, concat_axis=1, tiled=True)
    local_rows = tokens.shape[0]
    heads_here = key_cache.shape[1]
    head_size = key_cache.shape[3]
    query_group = query_weight.shape[1] // (heads_here * head_size)
    stream = tokens.astype(jnp.float32)
    normed_input = (
        stream
        / jnp.sqrt(jnp.sum(stream * stream, axis=-1, keepdims=True) / MODEL_WIDTH + EPS)
        * attn_gain
    ).astype(jnp.bfloat16)
    cosine, sine = rotary_tables(positions, head_size)
    query_rows, fresh_keys, fresh_values = lax.optimization_barrier(
        (
            jnp.dot(normed_input, query_weight, preferred_element_type=jnp.float32),
            jnp.dot(normed_input, key_matrix, preferred_element_type=jnp.float32),
            jnp.dot(normed_input, value_matrix, preferred_element_type=jnp.float32),
        )
    )
    query_rows = rotate(query_rows, cosine, sine, head_size).reshape(
        local_rows, heads_here, query_group, head_size
    )
    fresh_keys = rotate(fresh_keys, cosine, sine, head_size).reshape(
        local_rows, heads_here, head_size
    )
    fresh_values = fresh_values.astype(jnp.bfloat16).reshape(local_rows, heads_here, head_size)
    slots = jnp.arange(key_cache.shape[2], dtype=jnp.int32)[None, :]
    limit = cache_lengths[:, None]
    allowed = (slots < limit) & ((slots < SINKS) | (slots > limit - WINDOW))
    results = []
    for head in range(heads_here):
        results.append(
            attend(
                query_rows[:, head],
                key_cache[:, head],
                cached_values[:, head],
                fresh_keys[:, head],
                fresh_values[:, head],
                allowed,
            )
        )
    attended_rows = jnp.stack(results, axis=1).reshape(
        local_rows, heads_here * query_group * head_size
    )
    features = attended_rows.shape[1]
    weight_rows = lax.dynamic_slice_in_dim(output_weight, kv_place * features, features, 0)
    residual_rows = local_order(residual_in, req_place, req_size).astype(jnp.float32)
    partial_mix = jnp.dot(
        gather_rows(attended_rows, req_size),
        weight_rows,
        preferred_element_type=jnp.float32,
    ).astype(jnp.bfloat16)
    mixed = kv_sum(partial_mix, kv_place, kv_size)
    middle = residual_rows + mixed.astype(jnp.float32)
    scaled = (middle * mlp_gain).astype(jnp.bfloat16)
    squares = jnp.sum(middle * middle, axis=-1, keepdims=True)
    chain, total = feed_forward(scaled, squares, gate_weight, up_weight, down_weight, req_size)
    places = jnp.stack([req_place, lax.rem(kv_place, 2)]).astype(jnp.int32)
    send, kept = split_for_kv(chain, total, places, req_size, kv_size)
    value = kept.astype(jnp.float32) + kv_exchange(send, kv_size, 0).astype(jnp.float32)
    for bit in reversed(range(1, kv_size.bit_length() - 1)):
        half = value.shape[0] // 2
        mine = lax.rem(kv_place >> bit, 2)
        other = kv_exchange(
            lax.dynamic_slice_in_dim(value, (1 - mine) * half, half, 0).astype(jnp.bfloat16),
            kv_size,
            bit,
        )
        value = lax.dynamic_slice_in_dim(value, mine * half, half, 0) + other.astype(jnp.float32)
    per = req_size // kv_size
    base_rows = jnp.concatenate(
        [
            lax.dynamic_slice_in_dim(
                middle,
                local_spot(req_place, kv_place * per + i, req_size) * local_rows,
                local_rows,
                0,
            )
            for i in range(per)
        ],
        axis=0,
    )
    return (base_rows + value).astype(jnp.bfloat16)


def solution(mesh):
    return jax.shard_map(
        shards,
        mesh=mesh,
        in_specs=(
            P(None, "req"),
            P(),
            P(None, "kv"),
            P(None, "kv"),
            P(None, "kv"),
            P("req", "kv", None, None),
            P("req", "kv", None, None),
            P("req"),
            P("req"),
            P(None, "req"),
            P("req"),
            P("req", "kv"),
            P("req", "kv"),
            P("kv", "req"),
        ),
        out_specs=P("kv", "req"),
        check_vma=False,
    )
```

```python
import math

import jax
import jax.numpy as jnp
from jax import lax
from jax.experimental import pallas as pl
from jax.experimental.pallas import tpu as pltpu
from jax.sharding import PartitionSpec as P

MODEL_WIDTH = 4096
WINDOW = 512
SINKS = 4


EPS = 1e-05
THETA = 10000.0
JOINED = 4
SPLIT = 2
FETCH_VMEM = 32
EARLY_ROWS = (0, 128)
MIX_COST = 0
ATTENTION_VMEM = 56 * 1024 * 1024


def rotary_tables(places, head_size):
    half = head_size // 2
    freqs = jnp.exp(jnp.arange(half, dtype=jnp.float32) * (-2.0 * math.log(THETA) / head_size))
    angles = places.astype(jnp.float32)[:, None] * freqs[None, :]
    cosine, sine = jnp.cos(angles), jnp.sin(angles)
    return jnp.concatenate([cosine, cosine], axis=1), jnp.concatenate([-sine, sine], axis=1)


def attention(tokens, gain, weights, caches, tables, limits, heads_here, head_size):
    pieces, rows, depth = tokens.shape
    query_weight, key_matrix, value_matrix = weights
    keys, values = caches
    slots = keys.shape[2]
    heads = query_weight.shape[1] // head_size
    query_group = heads // heads_here
    members = min(rows, max(1, 128 // heads))
    lanes = members * heads
    factor = 1.0 / math.sqrt(head_size)

    def body(
        tokens_ref,
        gain_ref,
        query_far,
        key_far,
        value_far,
        keys_far,
        values_far,
        cosine_ref,
        sine_ref,
        limits_ref,
        out_ref,
        flat_ref,
        query_rows,
        key_rows,
        value_rows,
        mixed_rows,
        query_ref,
        key_ref,
        value_ref,
        keys_ref,
        values_ref,
        weight_sems,
        cache_sems,
    ):
        def weight_copies(piece):
            span = pl.ds(piece * depth, depth)
            return [
                pltpu.make_async_copy(far.at[span], near.at[span], weight_sems.at[piece, i])
                for i, (far, near) in enumerate(
                    ((query_far, query_ref), (key_far, key_ref), (value_far, value_ref))
                )
            ]

        def cache_copy(group, which):
            far, near = ((keys_far, keys_ref), (values_far, values_ref))[which]
            span = pl.ds(group * members, members)
            return pltpu.make_async_copy(far.at[span], near.at[span], cache_sems.at[group, which])

        for piece in range(pieces):
            for copy in weight_copies(piece):
                copy.start()
        for which in range(2):
            for group in range(rows // members):
                cache_copy(group, which).start()
        squares = jnp.zeros((rows, 1), jnp.float32)
        for piece in range(pieces):
            part = tokens_ref[piece].astype(jnp.float32)
            squares = squares + jnp.sum(part * part, axis=1, keepdims=True)
        scale = 1.0 / jnp.sqrt(squares / MODEL_WIDTH + EPS)
        sums = [None, None, None]
        for piece in range(pieces):
            span = slice(piece * depth, (piece + 1) * depth)
            part = tokens_ref[piece].astype(jnp.float32)
            normed = (part * scale * gain_ref[:, span]).astype(jnp.bfloat16)
            for copy in weight_copies(piece):
                copy.wait()
            for i, weight_ref in enumerate((query_ref, key_ref, value_ref)):
                product = jnp.dot(normed, weight_ref[span], preferred_element_type=jnp.float32)
                sums[i] = product if sums[i] is None else sums[i] + product
        cosine, sine = cosine_ref[...], sine_ref[...]

        def turned(value):
            swapped = jnp.concatenate(
                [value[:, head_size // 2 :], value[:, : head_size // 2]], axis=1
            )
            return (value * cosine + swapped * sine).astype(jnp.bfloat16).astype(jnp.float32)

        def put(ref, head, value):
            for group in range(rows // members):
                ref[pl.ds(group * lanes + head, members, stride=heads), :] = value[
                    group * members : (group + 1) * members
                ]

        for head in range(heads):
            own = head // query_group
            put(query_rows, head, turned(sums[0][:, head * head_size : (head + 1) * head_size]))
            if head % query_group == 0:
                new_key = turned(sums[1][:, own * head_size : (own + 1) * head_size])
                new_value = sums[2][:, own * head_size : (own + 1) * head_size]
                new_value = new_value.astype(jnp.bfloat16).astype(jnp.float32)
            put(key_rows, head, new_key)
            put(value_rows, head, new_value)
        slot = lax.broadcasted_iota(jnp.int32, (slots, lanes), 0)
        owner = lax.broadcasted_iota(jnp.int32, (head_size, lanes), 1) // query_group
        kept = []
        for group in range(rows // members):
            mine = slice(group * lanes, (group + 1) * lanes)
            query_columns = query_rows[mine].T
            own_score = (
                jnp.sum(query_columns * key_rows[mine].T, axis=0, keepdims=True) * factor
            )
            narrow = query_columns.astype(jnp.bfloat16)
            cache_copy(group, 0).wait()
            cut = slots // SPLIT
            parts = [None] * SPLIT
            for first in range(0, members, JOINED):
                pairs = [
                    (member, g)
                    for member in range(first, min(first + JOINED, members))
                    for g in range(heads_here)
                ]
                right = jnp.concatenate(
                    [
                        jnp.where(owner == member * heads_here + g, narrow, jnp.zeros_like(narrow))
                        for member, g in pairs
                    ],
                    axis=0,
                )
                for i in range(SPLIT):
                    left = jnp.concatenate(
                        [
                            keys_ref[group * members + member, g, i * cut : (i + 1) * cut]
                            for member, g in pairs
                        ],
                        axis=1,
                    )
                    product = jnp.dot(left, right, preferred_element_type=jnp.float32)
                    parts[i] = product if parts[i] is None else parts[i] + product
            scores = jnp.concatenate(parts, axis=0)
            lane_member = lax.broadcasted_iota(jnp.int32, (1, lanes), 1) // heads
            limit = jnp.zeros((1, lanes), jnp.int32)
            for member in range(members):
                limit = jnp.where(lane_member == member, limits_ref[group * members + member], limit)
            allowed = (slot < limit) & ((slot < SINKS) | (slot > limit - WINDOW))
            scores = jnp.where(allowed, scores * factor, -1e30)
            peak = jnp.maximum(jnp.max(scores, axis=0, keepdims=True), own_score)
            expo = jnp.where(allowed, jnp.exp(scores - peak), 0.0)
            own_expo = jnp.exp(own_score - peak)
            inverse = 1.0 / (jnp.sum(expo, axis=0, keepdims=True) + own_expo)
            shares = (expo * inverse).T
            own_share = (own_expo * inverse).astype(jnp.bfloat16).astype(jnp.float32)
            own_part = (
                jnp.broadcast_to(own_share, (head_size, lanes)).T * value_rows[mine]
            )
            kept.append((shares, own_part))
        for group, (shares, own_part) in enumerate(kept):
            cache_copy(group, 1).wait()
            for member in range(members):
                request = group * members + member
                span = slice(member * heads, (member + 1) * heads)
                wide = jnp.dot(
                    shares[span].astype(jnp.bfloat16),
                    jnp.concatenate([values_ref[request, g] for g in range(heads_here)], axis=1),
                    preferred_element_type=jnp.float32,
                )
                which = lax.broadcasted_iota(jnp.int32, (heads, head_size), 0) // query_group
                mixed = wide[:, :head_size]
                for g in range(1, heads_here):
                    mixed = jnp.where(which == g, wide[:, g * head_size : (g + 1) * head_size], mixed)
                mixed_rows[group * lanes + member * heads : group * lanes + (member + 1) * heads] = (
                    mixed + own_part[span]
                )
        for head in range(heads):
            for group in range(rows // members):
                flat_ref[group * members : (group + 1) * members, :] = mixed_rows[
                    pl.ds(group * lanes + head, members, stride=heads), :
                ]
            out_ref[:, head * head_size : (head + 1) * head_size] = flat_ref[...].astype(
                jnp.bfloat16
            )

    tall = pltpu.VMEM((rows * heads, head_size), jnp.float32)
    near = pl.BlockSpec(memory_space=pltpu.VMEM)
    return pl.pallas_call(
        body,
        out_shape=array((rows, heads * head_size), jnp.bfloat16),
        in_specs=[near, near, *[HBM] * 5, near, near, SCALARS],
        out_specs=pl.BlockSpec(memory_space=pltpu.VMEM),
        scratch_shapes=[
            pltpu.VMEM((rows, head_size), jnp.float32),
            *[tall] * 4,
            *[pltpu.VMEM(v.shape, v.dtype) for v in (*weights, *caches)],
            pltpu.SemaphoreType.DMA((pieces, 3)),
            pltpu.SemaphoreType.DMA((rows // members, 2)),
        ],
        compiler_params=pltpu.CompilerParams(vmem_limit_bytes=ATTENTION_VMEM),
    )(
        tokens,
        gain.reshape(1, -1),
        *weights,
        *caches,
        *tables,
        limits,
    )


def bit_reverse(value, bits):
    result = 0
    for bit in range(bits):
        result |= ((value >> bit) & 1) << (bits - 1 - bit)
    return result


def exchange(value, size, bit):
    return lax.ppermute(value, "req", [(i, i ^ (1 << bit)) for i in range(size)])


def local_spot(place, block, size):
    bits = size.bit_length() - 1
    other = place ^ block
    spot = jnp.int32(0)
    for bit in range(bits):
        spot = spot | (((other >> bit) & 1) << (bits - 1 - bit))
    return spot


def kv_exchange(value, size, bit):
    return lax.ppermute(value, "kv", [(i, i ^ (1 << bit)) for i in range(size)])


class Chain:
    def __init__(self, token):
        self.token = token

    def run(self, body, outs, ins, in_specs=None, after=(), scratch=(), vmem=32, cost=0):
        specs = list(in_specs or [None] * len(ins))
        specs = [pl.BlockSpec(memory_space=pltpu.VMEM) if v is None else v for v in specs]
        count = len(ins)
        unread = [self.token, *after]

        def kernel(*refs):
            body(*refs[:count], *refs[count + len(unread) :])

        results = pl.pallas_call(
            kernel,
            out_shape=outs,
            in_specs=[*specs, *[pl.BlockSpec(memory_space=pl.ANY)] * len(unread)],
            out_specs=[pl.BlockSpec(memory_space=pltpu.VMEM)] * len(outs),
            scratch_shapes=scratch,
            compiler_params=pltpu.CompilerParams(vmem_limit_bytes=vmem * 1024 * 1024),
            cost_estimate=pl.CostEstimate(flops=0, bytes_accessed=cost, transcendentals=0),
        )(*ins, *unread)
        self.token = results[0]
        return results


SCALARS = pl.BlockSpec(memory_space=pltpu.SMEM)
FAR = pl.BlockSpec(memory_space=pl.ANY)
HBM = pl.BlockSpec(memory_space=pltpu.HBM)


def array(shape, dtype):
    return jax.ShapeDtypeStruct(shape, dtype)


def corner(value):
    return value.reshape(-1, value.shape[-1])[:16, :128]


def tie(value, *after):
    def body(*refs):
        del refs

    return pl.pallas_call(
        body,
        out_shape=array(value.shape, value.dtype),
        in_specs=[FAR] * (1 + len(after)),
        out_specs=FAR,
        input_output_aliases={0: 0},
        cost_estimate=pl.CostEstimate(flops=0, bytes_accessed=0, transcendentals=0),
    )(value, *after)


def fetch(chain, places, features, output_weight, residual_in, req_size):
    total, columns = residual_in.shape
    bits = req_size.bit_length() - 1
    block = total // req_size

    def body(places_ref, weight_far, residual_ref, weight_ref, ordered_ref, sem):
        start = pl.multiple_of(places_ref[2] * features, features)
        copy = pltpu.make_async_copy(weight_far.at[pl.ds(start, features)], weight_ref, sem)
        copy.start()
        for spot in range(req_size):
            first = pl.multiple_of((places_ref[0] ^ bit_reverse(spot, bits)) * block, block)
            ordered_ref[spot * block : (spot + 1) * block] = residual_ref[pl.ds(first, block)]
        copy.wait()

    return chain.run(
        body,
        [
            array((features, columns), output_weight.dtype),
            array(residual_in.shape, residual_in.dtype),
        ],
        [places, output_weight, residual_in],
        [SCALARS, HBM, None],
        scratch=[pltpu.SemaphoreType.DMA(())],
        vmem=FETCH_VMEM,
    )


def mix(chain, rows, weight, req_size):
    block = rows.shape[0] // req_size
    back = local_from_pair(req_size, 0)

    def body(rows_ref, weight_ref, out_ref):
        left = jnp.concatenate([rows_ref[n * block : (n + 1) * block] for n in back], axis=0)
        out_ref[...] = jnp.dot(
            left, weight_ref[...], preferred_element_type=jnp.float32
        ).astype(jnp.bfloat16)

    out = array((rows.shape[0], weight.shape[1]), jnp.bfloat16)
    return chain.run(body, [out], [rows, weight], cost=MIX_COST)[0]


def half_sum(chain, places, rows, other):
    half, columns = rows.shape[0] // 2, rows.shape[1]

    def body(places_ref, rows_ref, other_ref, send_ref, part_ref):
        span = pl.ds(pl.multiple_of(places_ref[1] * half, half), half)
        part = rows_ref[span].astype(jnp.float32) + other_ref[span].astype(jnp.float32)
        part_ref[...] = part
        send_ref[...] = part.astype(jnp.bfloat16)

    return chain.run(
        body,
        [array((half, columns), jnp.bfloat16), array((half, columns), jnp.float32)],
        [places, rows, other],
        [SCALARS, None, None],
        cost=MIX_COST,
    )


def relay(chain, value):
    def body(value_ref, out_ref):
        out_ref[...] = value_ref[...]

    return chain.run(body, [array(value.shape, value.dtype)], [value])[0]


def next_sum(chain, part, other):
    def body(part_ref, other_ref, send_ref, sum_ref):
        total = part_ref[...] + other_ref[...].astype(jnp.float32)
        sum_ref[...] = total
        send_ref[...] = total.astype(jnp.bfloat16)

    return chain.run(
        body, [array(part.shape, jnp.bfloat16), array(part.shape, jnp.float32)], [part, other]
    )


def middle_half(chain, places, mixed, residual_rows, gain):
    half, columns = mixed.shape

    def body(places_ref, mixed_ref, residual_ref, gain_ref, out_ref):
        span = pl.ds(pl.multiple_of(places_ref[1] * half, half), half)
        middle = residual_ref[span].astype(jnp.float32) + mixed_ref[...].astype(jnp.float32)
        out_ref[:, :columns] = (middle * gain_ref[...]).astype(jnp.bfloat16)
        out_ref[:, columns:] = jnp.broadcast_to(
            jnp.sum(middle * middle, axis=1, keepdims=True), (half, 128)
        ).astype(jnp.bfloat16)

    return chain.run(
        body,
        [array((half, columns + 128), jnp.bfloat16)],
        [places, mixed, residual_rows, gain],
        [SCALARS, None, None, None],
    )[0]


def middle_rows(chain, places, mixed, other, residual_rows, gain):
    half, columns = mixed.shape
    rows = 2 * half

    def body(places_ref, mixed_ref, other_ref, residual_ref, gain_ref, scaled_ref, middle_ref, squares_ref):
        for mine, ref in ((0, mixed_ref), (1, other_ref)):
            first = places_ref[1] if mine == 0 else 1 - places_ref[1]
            span = pl.ds(pl.multiple_of(first * half, half), half)
            middle = residual_ref[span].astype(jnp.float32) + ref[...].astype(jnp.float32)
            middle_ref[span] = middle
            scaled_ref[span] = (middle * gain_ref[...]).astype(jnp.bfloat16)
            squares_ref[span] = jnp.broadcast_to(
                jnp.sum(middle * middle, axis=1, keepdims=True), (half, 128)
            )

    return chain.run(
        body,
        [
            array((rows, columns), jnp.bfloat16),
            array((rows, columns), jnp.float32),
            array((rows, 128), jnp.float32),
        ],
        [places, mixed, other, residual_rows, gain],
        [SCALARS, None, None, None, None],
    )


def project(chain, scaled, squares, gate, up, start, width):
    half = scaled.shape[0] // 2

    def body(scaled_ref, gate_ref, up_ref, squares_ref, send_ref, keep_ref):
        for first, out_ref in ((half, send_ref), (0, keep_ref)):
            left = scaled_ref[first : first + half]
            for i, weight_ref in enumerate((gate_ref, up_ref)):
                out_ref[:, i * width : (i + 1) * width] = jnp.dot(
                    left, weight_ref[:, start : start + width], preferred_element_type=jnp.float32
                ).astype(jnp.bfloat16)

            out_ref[:, 2 * width :] = squares_ref[first : first + half].astype(jnp.bfloat16)

    out = array((half, 2 * width + 128), jnp.bfloat16)
    return chain.run(body, [out, out], [scaled, gate, up, squares])


def pair_order(size, pair):
    bits = size.bit_length() - 1
    sums = [bit for bit in range(bits) if bit != pair]
    spots = []
    for n in range(size):
        spot = (n & 1) << (bits - 1 - pair)
        for i, bit in enumerate(sums):
            spot |= ((n >> (bits - 1 - i)) & 1) << (bits - 1 - bit)
        spots.append(spot)
    return spots


def local_from_pair(size, pair):
    order = pair_order(size, pair)
    return [order.index(spot) for spot in range(size)]


def project_pair(chain, places, scaled, squares, far, got, gate, up, pair, area, start, skip, width, req_size):
    rows, depth = scaled.shape
    half, block = rows // 2, rows // req_size
    order = pair_order(req_size, pair)
    flip = 1 << (req_size.bit_length() - 2 - pair)
    cut = got[0].shape[0] - depth
    total = 2 * width + (0 if squares is None else 128)

    def body(places_ref, scaled_ref, far_ref, away_ref, *refs):
        early_ref, late_ref = refs[:2]
        weight_fars = refs[2:4]
        send_ref, keep_ref, all_far, weights, sems = refs[-5:]
        mine = lax.rem(places_ref[0] // (1 << pair), 2)
        columns = pl.ds(pl.multiple_of(start + mine * area + skip, 128), width)
        copies = [
            pltpu.make_async_copy(weight_fars[i].at[:, columns], weights.at[i], sems.at[i])
            for i in range(2)
        ]
        for copy in copies:
            copy.start()
        for away, ref in ((0, far_ref), (1, away_ref)):
            first = 1 - places_ref[1] if away else places_ref[1]
            all_far[pl.ds(pl.multiple_of(first * half, half), half)] = ref[...]
        outs = ((order[req_size // 2 :], send_ref), (order[: req_size // 2], keep_ref))

        def take(ref, spots, span, change=0):
            return jnp.concatenate(
                [
                    ref[(spot ^ change) * block : ((spot ^ change) + 1) * block, span]
                    for spot in spots
                ],
                axis=0,
            )

        others = []
        for spots, out_ref in outs:
            for i in range(2):
                spans = [(early_ref, 0, 0, depth)]
                if i == 1:
                    spans = [(early_ref, depth, 0, cut), (late_ref, 0, cut, depth)]
                product = None
                for ref, top, begin, end in spans:
                    if end > begin:
                        part = jnp.dot(
                            take(all_far, spots, slice(begin, end), flip),
                            ref[top : top + end - begin, skip : skip + width],
                            preferred_element_type=jnp.float32,
                        )
                        product = part if product is None else product + part
                others.append(product)
            if squares is not None:
                out_ref[:, 2 * width :] = (
                    take(refs[4], spots, slice(0, 128))
                    + take(all_far, spots, slice(depth, depth + 128), flip).astype(jnp.float32)
                ).astype(jnp.bfloat16)
        for copy in copies:
            copy.wait()
        for j, (spots, out_ref) in enumerate(outs):
            for i in range(2):
                near = jnp.dot(
                    take(scaled_ref, spots, slice(0, depth)),
                    weights[i],
                    preferred_element_type=jnp.float32,
                )
                out_ref[:, i * width : (i + 1) * width] = (near + others[2 * j + i]).astype(
                    jnp.bfloat16
                )

    ins = [places, scaled, *far, *got, gate, up] + ([] if squares is None else [squares])
    specs = [SCALARS, None, None, None, None, None, HBM, HBM] + [None] * (len(ins) - 8)
    out = array((half, total), jnp.bfloat16)
    return chain.run(
        body,
        [out, out],
        ins,
        specs,
        scratch=[
            pltpu.VMEM((rows, depth + 128), jnp.bfloat16),
            pltpu.VMEM((2, depth, width), gate.dtype),
            pltpu.SemaphoreType.DMA((2,)),
        ],
    )


def add_halve(chain, other, kept):
    half = kept.shape[0] // 2

    def body(other_ref, kept_ref, send_ref, keep_ref):
        for start, out_ref in ((half, send_ref), (0, keep_ref)):
            rows = slice(start, start + half)
            out_ref[...] = (
                other_ref[rows].astype(jnp.float32) + kept_ref[rows].astype(jnp.float32)
            ).astype(jnp.bfloat16)

    out = array((half, kept.shape[1]), jnp.bfloat16)
    return chain.run(body, [out, out], [other, kept])


def activate(chain, other, kept, inverse, width):
    rows = kept.shape[0]
    first = inverse is None

    def body(other_ref, kept_ref, *refs):
        def total(columns):
            return other_ref[:, columns].astype(jnp.float32) + kept_ref[:, columns].astype(
                jnp.float32
            )

        if first:
            hidden_ref, inverse_ref = refs
            scale = 1.0 / jnp.sqrt(total(slice(2 * width, 2 * width + 128)) / MODEL_WIDTH + EPS)
            inverse_ref[...] = scale
        else:
            scale_ref, hidden_ref = refs
            scale = scale_ref[:rows]
        scale = scale[:, :1]
        gate = total(slice(0, width)) * scale
        up = total(slice(width, 2 * width)) * scale
        hidden_ref[...] = (gate / (1.0 + jnp.exp(-gate)) * up).astype(jnp.bfloat16)

    outs = [array((rows, width), jnp.bfloat16)]
    ins = [other, kept]
    if first:
        outs.append(array((rows, 128), jnp.float32))
    else:
        ins.append(inverse)
    results = chain.run(body, outs, ins)
    return results if first else (results[0], inverse)


def join(chain, kept, other, after=()):
    rows = kept.shape[0]

    def body(kept_ref, other_ref, out_ref):
        out_ref[:rows] = kept_ref[...]
        out_ref[rows:] = other_ref[...]

    return chain.run(
        body, [array((2 * rows, kept.shape[1]), kept.dtype)], [kept, other], after=after
    )[0]


def lower(chain, places, kept, other, down, pair, area, start, skip, width, carried, req_size):
    columns = down.shape[1]
    paired = pair is not None
    rows = kept.shape[0] * (1 if paired else 2)
    half, block = rows // 2, rows // req_size
    back = local_from_pair(req_size, pair) if paired else None

    def body(places_ref, kept_ref, other_ref, down_ref, *refs):
        out_ref = refs[-1]

        def product(left, first):
            return jnp.dot(
                left, down_ref[pl.ds(first, width)], preferred_element_type=jnp.float32
            )

        def take(ref, flip):
            return jnp.concatenate(
                [ref[(n ^ flip) * block : ((n ^ flip) + 1) * block] for n in back], axis=0
            )

        if paired:
            mine = lax.rem(places_ref[0] // (1 << pair), 2)
            total = product(take(kept_ref, 0), pl.multiple_of(start + mine * area + skip, 128))
            total = total + product(
                take(other_ref, 1), pl.multiple_of(start + (1 - mine) * area + skip, 128)
            )
            out_ref[...] = total if carried is None else refs[0][...] + total
        else:
            for first, ref in ((0, kept_ref), (half, other_ref)):
                span = slice(first, first + half)
                total = product(ref[...], start)
                out_ref[span] = total if carried is None else refs[0][span] + total

    ins = [places, kept, other, down] + ([] if carried is None else [carried])
    return chain.run(
        body, [array((rows, columns), jnp.float32)], ins, [SCALARS] + [None] * (len(ins) - 1)
    )[0]


def split_for_kv(chain, total, places, req_size, kv_size):
    rows, columns = total.shape
    bits = req_size.bit_length() - 1
    block = rows // req_size
    per = req_size // kv_size

    def body(places_ref, total_ref, send_ref, keep_ref):
        req_place, mine = places_ref[0], places_ref[1]
        for spot in range(req_size):
            actual = req_place ^ bit_reverse(spot, bits)
            owner = actual // per
            start = pl.multiple_of(((owner // 2) * per + actual % per) * block, block)
            value = total_ref[spot * block : (spot + 1) * block].astype(jnp.bfloat16)

            @pl.when(owner % 2 == mine)
            def _():
                keep_ref[pl.ds(start, block)] = value

            @pl.when(owner % 2 != mine)
            def _():
                send_ref[pl.ds(start, block)] = value

    out = array((rows // 2, columns), jnp.bfloat16)
    return chain.run(
        body,
        [out, out],
        [places, total],
        [SCALARS, None],
    )


class Chunk:
    def __init__(self, pair, start, area, skip, width, bits):
        self.pair, self.start, self.area, self.skip, self.width = pair, start, area, skip, width
        self.sums = [bit for bit in range(bits) if bit != pair]
        self.gathers = [*reversed(self.sums), *([] if pair is None else [pair])]
        self.kept = self.moving = None


def areas_of(columns):
    tiles = columns // 128
    return tiles // 4 * 128, tiles // 4 * 128


def plan(columns, bits):
    first, second = areas_of(columns)
    rest = columns - 2 * first - 2 * second
    chunks = [Chunk(0, 0, first, 0, first, bits), Chunk(1, 2 * first, second, 0, second, bits)]
    if rest:
        chunks.insert(0, Chunk(None, columns - rest, 0, 0, rest, bits))
    stages = 2 * bits + 1
    tasks = [
        (i, stage)
        for stage in range(stages)
        for i, chunk in enumerate(chunks)
        if stage <= len(chunk.sums) + len(chunk.gathers)
    ]
    return chunks, tasks


def feed_forward(chain, places, scaled, squares, far_parts, gots, gate, up, down, req_size, kv_size):
    bits = req_size.bit_length() - 1
    total = None
    inverses, fars = {}, {}
    chunks, tasks = plan(gate.shape[1], bits)
    for i, stage in tasks:
        chunk = chunks[i]
        pair, sums, gathers = chunk.pair, chunk.sums, chunk.gathers
        if stage == 0:
            if pair is not None:
                if pair not in fars:
                    far = relay(chain, far_parts[pair])
                    fars[pair] = (far, kv_exchange(far, kv_size, 0))
                send, chunk.kept = project_pair(
                    chain,
                    places,
                    scaled,
                    squares if chunk.skip == 0 else None,
                    fars[pair],
                    gots[pair],
                    gate,
                    up,
                    pair,
                    chunk.area,
                    chunk.start,
                    chunk.skip,
                    chunk.width,
                    req_size,
                )
            else:
                send, chunk.kept = project(
                    chain, scaled, squares, gate, up, chunk.start, chunk.width
                )
            chunk.moving = exchange(send, req_size, sums[0])
        elif stage < len(sums):
            send, chunk.kept = add_halve(chain, chunk.moving, chunk.kept)
            chunk.moving = exchange(send, req_size, sums[stage])
        elif stage == len(sums):
            chunk.kept, inverses[pair] = activate(
                chain,
                chunk.moving,
                chunk.kept,
                inverses.get(pair),
                chunk.width,
            )
            chunk.moving = exchange(chunk.kept, req_size, gathers[0])
        elif stage < len(sums) + len(gathers):
            chunk.kept = join(chain, chunk.kept, chunk.moving)
            chunk.moving = exchange(chunk.kept, req_size, gathers[stage - len(sums)])
        else:
            total = lower(
                chain,
                places,
                chunk.kept,
                chunk.moving,
                down,
                pair,
                chunk.area,
                chunk.start,
                chunk.skip,
                chunk.width,
                total,
                req_size,
            )
    return total


def shards(
    residual_in,
    attn_gain,
    query_weight,
    key_matrix,
    value_matrix,
    key_cache,
    cached_values,
    cache_lengths,
    positions,
    output_weight,
    mlp_gain,
    gate_weight,
    up_weight,
    down_weight,
):
    req_size = lax.axis_size("req")
    kv_size = lax.axis_size("kv")
    req_place = lax.axis_index("req")
    kv_place = lax.axis_index("kv")
    local_rows = residual_in.shape[0] // req_size
    heads_here, head_size = key_cache.shape[1], key_cache.shape[3]
    tokens = lax.all_to_all(
        residual_in.reshape(req_size, local_rows, -1), "req", split_axis=0, concat_axis=0
    )
    attended_rows = attention(
        tokens,
        attn_gain,
        (query_weight, key_matrix, value_matrix),
        (key_cache, cached_values),
        rotary_tables(positions, head_size),
        cache_lengths,
        heads_here,
        head_size,
    )
    features = attended_rows.shape[1]
    places = jnp.stack([req_place, lax.rem(kv_place, 2), kv_place]).astype(jnp.int32)
    areas = areas_of(gate_weight.shape[1])
    theirs = []
    for pair, area in enumerate(areas):
        first = 2 * sum(areas[:pair]) + (1 - lax.rem(req_place // (1 << pair), 2)) * area
        slices = [lax.dynamic_slice_in_dim(v, first, area, 1) for v in (gate_weight, up_weight)]
        cut = EARLY_ROWS[pair] * gate_weight.shape[0] // 512
        early = jnp.concatenate([slices[0], slices[1][:cut]], axis=0) if cut else slices[0]
        theirs.append((early, slices[1][cut:]))
    start = corner(tokens)
    gots = [
        [exchange(tie(theirs[0][0], start, theirs[0][1], *theirs[1]), req_size, 0)],
        [exchange(tie(theirs[1][0], start), req_size, 1)],
    ]
    chain = Chain(attended_rows)
    output_rows, residual_rows = fetch(
        chain, places, features, output_weight, residual_in, req_size
    )
    gathered = attended_rows
    bits = req_size.bit_length() - 1
    for bit in (0, *reversed(range(1, bits))):
        other = exchange(gathered, req_size, bit)
        gathered = join(chain, gathered, other, [gots[0][0], gots[1][0]] if bit == 0 else [])
        if bit == 0:
            gots[0].append(exchange(tie(theirs[0][1], corner(gathered)), req_size, 0))
    gots[1].append(exchange(tie(theirs[1][1], corner(gathered)), req_size, 1))
    partial_mix = mix(chain, gathered, output_rows, req_size)
    gain = mlp_gain.reshape(1, -1)
    send, part = half_sum(chain, places, partial_mix, kv_exchange(partial_mix, kv_size, 0))
    for bit in range(1, kv_size.bit_length() - 1):
        send, part = next_sum(chain, part, kv_exchange(send, kv_size, bit))
    beside = kv_exchange(send, kv_size, 0)
    near_part = middle_half(chain, places, send, residual_rows, gain)
    far_parts = [exchange(near_part, req_size, pair) for pair in range(2)]
    scaled, middle, squares = middle_rows(chain, places, send, beside, residual_rows, gain)
    gate, up, down = gate_weight, up_weight, down_weight
    total = feed_forward(
        chain, places, scaled, squares, far_parts, gots, gate, up, down, req_size, kv_size
    )
    send, kept = split_for_kv(chain, total, places, req_size, kv_size)
    value = kept.astype(jnp.float32) + kv_exchange(send, kv_size, 0).astype(jnp.float32)
    for bit in reversed(range(1, kv_size.bit_length() - 1)):
        half = value.shape[0] // 2
        mine = lax.rem(kv_place >> bit, 2)
        other = kv_exchange(
            lax.dynamic_slice_in_dim(value, (1 - mine) * half, half, 0).astype(jnp.bfloat16),
            kv_size,
            bit,
        )
        value = lax.dynamic_slice_in_dim(value, mine * half, half, 0) + other.astype(jnp.float32)
    per = req_size // kv_size
    base_rows = jnp.concatenate(
        [
            lax.dynamic_slice_in_dim(
                middle,
                local_spot(req_place, kv_place * per + i, req_size) * local_rows,
                local_rows,
                0,
            )
            for i in range(per)
        ],
        axis=0,
    )
    return (base_rows + value).astype(jnp.bfloat16)


def solution(mesh):
    return jax.shard_map(
        shards,
        mesh=mesh,
        in_specs=(
            P(None, "req"),
            P(),
            P(None, "kv"),
            P(None, "kv"),
            P(None, "kv"),
            P("req", "kv", None, None),
            P("req", "kv", None, None),
            P("req"),
            P("req"),
            P(None, "req"),
            P("req"),
            P("req", "kv"),
            P("req", "kv"),
            P("kv", "req"),
        ),
        out_specs=P("kv", "req"),
        check_vma=False,
    )
```

```python
import math

import jax
import jax.numpy as jnp
from jax import lax
from jax.experimental import pallas as pl
from jax.experimental.pallas import tpu as pltpu
from jax.sharding import PartitionSpec as P

MODEL_WIDTH = 4096
WINDOW = 512
SINKS = 4


EPS = 1e-05
THETA = 10000.0
JOINED = 4
SPLIT = 2
FETCH_VMEM = 32
EARLY_ROWS = (256, 0)
PRELOAD_VMEM = 40 * 1024 * 1024
ATTENTION_VMEM = 32 * 1024 * 1024


def rotary_tables(places, head_size):
    half = head_size // 2
    freqs = jnp.exp(jnp.arange(half, dtype=jnp.float32) * (-2.0 * math.log(THETA) / head_size))
    angles = places.astype(jnp.float32)[:, None] * freqs[None, :]
    cosine, sine = jnp.cos(angles), jnp.sin(angles)
    return jnp.concatenate([cosine, cosine], axis=1), jnp.concatenate([-sine, sine], axis=1)


def attention(tokens, gain, weights, caches, tables, limits, heads_here, head_size):
    pieces, rows, depth = tokens.shape
    query_weight, key_matrix, value_matrix = weights
    keys, values = caches
    slots = keys.shape[2]
    heads = query_weight.shape[1] // head_size
    query_group = heads // heads_here
    members = min(rows, max(1, 128 // heads))
    lanes = members * heads
    factor = 1.0 / math.sqrt(head_size)

    def body(
        tokens_ref,
        gain_ref,
        query_ref,
        key_ref,
        value_ref,
        keys_far,
        values_far,
        cosine_ref,
        sine_ref,
        limits_ref,
        out_ref,
        flat_ref,
        query_rows,
        key_rows,
        value_rows,
        mixed_rows,
        keys_ref,
        values_ref,
        cache_sems,
    ):
        def cache_copy(group, which):
            far, near = ((keys_far, keys_ref), (values_far, values_ref))[which]
            span = pl.ds(group * members, members)
            return pltpu.make_async_copy(far.at[span], near.at[span], cache_sems.at[group, which])

        for which in range(2):
            for group in range(rows // members):
                cache_copy(group, which).start()
        squares = jnp.zeros((rows, 1), jnp.float32)
        for piece in range(pieces):
            part = tokens_ref[piece].astype(jnp.float32)
            squares = squares + jnp.sum(part * part, axis=1, keepdims=True)
        scale = 1.0 / jnp.sqrt(squares / MODEL_WIDTH + EPS)
        sums = [None, None, None]
        for piece in range(pieces):
            span = slice(piece * depth, (piece + 1) * depth)
            part = tokens_ref[piece].astype(jnp.float32)
            normed = (part * scale * gain_ref[:, span]).astype(jnp.bfloat16)
            for i, weight_ref in enumerate((query_ref, key_ref, value_ref)):
                product = jnp.dot(normed, weight_ref[span], preferred_element_type=jnp.float32)
                sums[i] = product if sums[i] is None else sums[i] + product
        cosine, sine = cosine_ref[...], sine_ref[...]

        def turned(value):
            swapped = jnp.concatenate(
                [value[:, head_size // 2 :], value[:, : head_size // 2]], axis=1
            )
            return (value * cosine + swapped * sine).astype(jnp.bfloat16).astype(jnp.float32)

        def put(ref, head, value):
            for group in range(rows // members):
                ref[pl.ds(group * lanes + head, members, stride=heads), :] = value[
                    group * members : (group + 1) * members
                ]

        for head in range(heads):
            own = head // query_group
            put(query_rows, head, turned(sums[0][:, head * head_size : (head + 1) * head_size]))
            if head % query_group == 0:
                new_key = turned(sums[1][:, own * head_size : (own + 1) * head_size])
                new_value = sums[2][:, own * head_size : (own + 1) * head_size]
                new_value = new_value.astype(jnp.bfloat16).astype(jnp.float32)
            put(key_rows, head, new_key)
            put(value_rows, head, new_value)
        slot = lax.broadcasted_iota(jnp.int32, (slots, lanes), 0)
        owner = lax.broadcasted_iota(jnp.int32, (head_size, lanes), 1) // query_group
        kept = []
        for group in range(rows // members):
            mine = slice(group * lanes, (group + 1) * lanes)
            query_columns = query_rows[mine].T
            own_score = (
                jnp.sum(query_columns * key_rows[mine].T, axis=0, keepdims=True) * factor
            )
            narrow = query_columns.astype(jnp.bfloat16)
            cache_copy(group, 0).wait()
            cut = slots // SPLIT
            parts = [None] * SPLIT
            for first in range(0, members, JOINED):
                pairs = [
                    (member, g)
                    for member in range(first, min(first + JOINED, members))
                    for g in range(heads_here)
                ]
                right = jnp.concatenate(
                    [
                        jnp.where(owner == member * heads_here + g, narrow, jnp.zeros_like(narrow))
                        for member, g in pairs
                    ],
                    axis=0,
                )
                for i in range(SPLIT):
                    left = jnp.concatenate(
                        [
                            keys_ref[group * members + member, g, i * cut : (i + 1) * cut]
                            for member, g in pairs
                        ],
                        axis=1,
                    )
                    product = jnp.dot(left, right, preferred_element_type=jnp.float32)
                    parts[i] = product if parts[i] is None else parts[i] + product
            scores = jnp.concatenate(parts, axis=0)
            lane_member = lax.broadcasted_iota(jnp.int32, (1, lanes), 1) // heads
            limit = jnp.zeros((1, lanes), jnp.int32)
            for member in range(members):
                limit = jnp.where(lane_member == member, limits_ref[group * members + member], limit)
            allowed = (slot < limit) & ((slot < SINKS) | (slot > limit - WINDOW))
            scores = jnp.where(allowed, scores * factor, -1e30)
            peak = jnp.maximum(jnp.max(scores, axis=0, keepdims=True), own_score)
            expo = jnp.where(allowed, jnp.exp(scores - peak), 0.0)
            own_expo = jnp.exp(own_score - peak)
            inverse = 1.0 / (jnp.sum(expo, axis=0, keepdims=True) + own_expo)
            shares = (expo * inverse).T
            own_share = (own_expo * inverse).astype(jnp.bfloat16).astype(jnp.float32)
            own_part = (
                jnp.broadcast_to(own_share, (head_size, lanes)).T * value_rows[mine]
            )
            kept.append((shares, own_part))
        for group, (shares, own_part) in enumerate(kept):
            cache_copy(group, 1).wait()
            for member in range(members):
                request = group * members + member
                span = slice(member * heads, (member + 1) * heads)
                wide = jnp.dot(
                    shares[span].astype(jnp.bfloat16),
                    jnp.concatenate([values_ref[request, g] for g in range(heads_here)], axis=1),
                    preferred_element_type=jnp.float32,
                )
                which = lax.broadcasted_iota(jnp.int32, (heads, head_size), 0) // query_group
                mixed = wide[:, :head_size]
                for g in range(1, heads_here):
                    mixed = jnp.where(which == g, wide[:, g * head_size : (g + 1) * head_size], mixed)
                mixed_rows[group * lanes + member * heads : group * lanes + (member + 1) * heads] = (
                    mixed + own_part[span]
                )
        for head in range(heads):
            for group in range(rows // members):
                flat_ref[group * members : (group + 1) * members, :] = mixed_rows[
                    pl.ds(group * lanes + head, members, stride=heads), :
                ]
            out_ref[:, head * head_size : (head + 1) * head_size] = flat_ref[...].astype(
                jnp.bfloat16
            )

    tall = pltpu.VMEM((rows * heads, head_size), jnp.float32)
    near = pl.BlockSpec(memory_space=pltpu.VMEM)
    return pl.pallas_call(
        body,
        out_shape=array((rows, heads * head_size), jnp.bfloat16),
        in_specs=[*[near] * 5, HBM, HBM, near, near, SCALARS],
        out_specs=pl.BlockSpec(memory_space=pltpu.VMEM),
        scratch_shapes=[
            pltpu.VMEM((rows, head_size), jnp.float32),
            *[tall] * 4,
            *[pltpu.VMEM(v.shape, v.dtype) for v in caches],
            pltpu.SemaphoreType.DMA((rows // members, 2)),
        ],
        compiler_params=pltpu.CompilerParams(vmem_limit_bytes=ATTENTION_VMEM),
    )(
        tokens,
        gain.reshape(1, -1),
        *weights,
        *caches,
        *tables,
        limits,
    )


def bit_reverse(value, bits):
    result = 0
    for bit in range(bits):
        result |= ((value >> bit) & 1) << (bits - 1 - bit)
    return result


def exchange(value, size, bit):
    return lax.ppermute(value, "req", [(i, i ^ (1 << bit)) for i in range(size)])


def local_spot(place, block, size):
    bits = size.bit_length() - 1
    other = place ^ block
    spot = jnp.int32(0)
    for bit in range(bits):
        spot = spot | (((other >> bit) & 1) << (bits - 1 - bit))
    return spot


def kv_exchange(value, size, bit):
    return lax.ppermute(value, "kv", [(i, i ^ (1 << bit)) for i in range(size)])


class Chain:
    def __init__(self, token):
        self.token = token

    def run(self, body, outs, ins, in_specs=None, after=(), scratch=(), vmem=32, cost=0):
        specs = list(in_specs or [None] * len(ins))
        specs = [pl.BlockSpec(memory_space=pltpu.VMEM) if v is None else v for v in specs]
        count = len(ins)
        unread = [self.token, *after]

        def kernel(*refs):
            body(*refs[:count], *refs[count + len(unread) :])

        results = pl.pallas_call(
            kernel,
            out_shape=outs,
            in_specs=[*specs, *[pl.BlockSpec(memory_space=pl.ANY)] * len(unread)],
            out_specs=[pl.BlockSpec(memory_space=pltpu.VMEM)] * len(outs),
            scratch_shapes=scratch,
            compiler_params=pltpu.CompilerParams(vmem_limit_bytes=vmem * 1024 * 1024),
            cost_estimate=pl.CostEstimate(flops=0, bytes_accessed=cost, transcendentals=0),
        )(*ins, *unread)
        self.token = results[0]
        return results


SCALARS = pl.BlockSpec(memory_space=pltpu.SMEM)
FAR = pl.BlockSpec(memory_space=pl.ANY)
HBM = pl.BlockSpec(memory_space=pltpu.HBM)


def array(shape, dtype):
    return jax.ShapeDtypeStruct(shape, dtype)


def corner(value):
    return value.reshape(-1, value.shape[-1])[:16, :128]


def tie(value, *after):
    def body(*refs):
        del refs

    return pl.pallas_call(
        body,
        out_shape=array(value.shape, value.dtype),
        in_specs=[FAR] * (1 + len(after)),
        out_specs=FAR,
        input_output_aliases={0: 0},
        cost_estimate=pl.CostEstimate(flops=0, bytes_accessed=0, transcendentals=0),
    )(value, *after)


def fetch(chain, places, features, output_weight, residual_in, req_size):
    total, columns = residual_in.shape
    bits = req_size.bit_length() - 1
    block = total // req_size

    def body(places_ref, weight_far, residual_ref, weight_ref, ordered_ref, sem):
        start = pl.multiple_of(places_ref[2] * features, features)
        copy = pltpu.make_async_copy(weight_far.at[pl.ds(start, features)], weight_ref, sem)
        copy.start()
        for spot in range(req_size):
            first = pl.multiple_of((places_ref[0] ^ bit_reverse(spot, bits)) * block, block)
            ordered_ref[spot * block : (spot + 1) * block] = residual_ref[pl.ds(first, block)]
        copy.wait()

    return chain.run(
        body,
        [
            array((features, columns), output_weight.dtype),
            array(residual_in.shape, residual_in.dtype),
        ],
        [places, output_weight, residual_in],
        [SCALARS, HBM, None],
        scratch=[pltpu.SemaphoreType.DMA(())],
        vmem=FETCH_VMEM,
    )


def mix(chain, rows, weight):
    def body(rows_ref, weight_ref, out_ref):
        out_ref[...] = jnp.dot(
            rows_ref[...], weight_ref[...], preferred_element_type=jnp.float32
        ).astype(jnp.bfloat16)

    out = array((rows.shape[0], weight.shape[1]), jnp.bfloat16)
    return chain.run(body, [out], [rows, weight])[0]


def half_sum(chain, places, rows, other):
    half, columns = rows.shape[0] // 2, rows.shape[1]

    def body(places_ref, rows_ref, other_ref, send_ref, part_ref):
        span = pl.ds(pl.multiple_of(places_ref[1] * half, half), half)
        part = rows_ref[span].astype(jnp.float32) + other_ref[span].astype(jnp.float32)
        part_ref[...] = part
        send_ref[...] = part.astype(jnp.bfloat16)

    return chain.run(
        body,
        [array((half, columns), jnp.bfloat16), array((half, columns), jnp.float32)],
        [places, rows, other],
        [SCALARS, None, None],
    )


def relay(chain, value):
    def body(value_ref, out_ref):
        out_ref[...] = value_ref[...]

    return chain.run(body, [array(value.shape, value.dtype)], [value])[0]


def next_sum(chain, part, other):
    def body(part_ref, other_ref, send_ref, sum_ref):
        total = part_ref[...] + other_ref[...].astype(jnp.float32)
        sum_ref[...] = total
        send_ref[...] = total.astype(jnp.bfloat16)

    return chain.run(
        body, [array(part.shape, jnp.bfloat16), array(part.shape, jnp.float32)], [part, other]
    )


def middle_half(chain, places, mixed, residual_rows, gain):
    half, columns = mixed.shape

    def body(places_ref, mixed_ref, residual_ref, gain_ref, out_ref):
        span = pl.ds(pl.multiple_of(places_ref[1] * half, half), half)
        middle = residual_ref[span].astype(jnp.float32) + mixed_ref[...].astype(jnp.float32)
        out_ref[:, :columns] = (middle * gain_ref[...]).astype(jnp.bfloat16)
        out_ref[:, columns:] = jnp.broadcast_to(
            jnp.sum(middle * middle, axis=1, keepdims=True), (half, 128)
        ).astype(jnp.bfloat16)

    return chain.run(
        body,
        [array((half, columns + 128), jnp.bfloat16)],
        [places, mixed, residual_rows, gain],
        [SCALARS, None, None, None],
    )[0]


def middle_rows(chain, places, mixed, other, residual_rows, gain):
    half, columns = mixed.shape
    rows = 2 * half

    def body(places_ref, mixed_ref, other_ref, residual_ref, gain_ref, scaled_ref, middle_ref, squares_ref):
        for mine, ref in ((0, mixed_ref), (1, other_ref)):
            first = places_ref[1] if mine == 0 else 1 - places_ref[1]
            span = pl.ds(pl.multiple_of(first * half, half), half)
            middle = residual_ref[span].astype(jnp.float32) + ref[...].astype(jnp.float32)
            middle_ref[span] = middle
            scaled_ref[span] = (middle * gain_ref[...]).astype(jnp.bfloat16)
            squares_ref[span] = jnp.broadcast_to(
                jnp.sum(middle * middle, axis=1, keepdims=True), (half, 128)
            )

    return chain.run(
        body,
        [
            array((rows, columns), jnp.bfloat16),
            array((rows, columns), jnp.float32),
            array((rows, 128), jnp.float32),
        ],
        [places, mixed, other, residual_rows, gain],
        [SCALARS, None, None, None, None],
    )


def project(chain, scaled, squares, gate, up, start, width):
    half = scaled.shape[0] // 2

    def body(scaled_ref, gate_ref, up_ref, squares_ref, send_ref, keep_ref):
        for first, out_ref in ((half, send_ref), (0, keep_ref)):
            left = scaled_ref[first : first + half]
            for i, weight_ref in enumerate((gate_ref, up_ref)):
                out_ref[:, i * width : (i + 1) * width] = jnp.dot(
                    left, weight_ref[:, start : start + width], preferred_element_type=jnp.float32
                ).astype(jnp.bfloat16)

            out_ref[:, 2 * width :] = squares_ref[first : first + half].astype(jnp.bfloat16)

    out = array((half, 2 * width + 128), jnp.bfloat16)
    return chain.run(body, [out, out], [scaled, gate, up, squares])


def pair_order(size, pair):
    bits = size.bit_length() - 1
    sums = [bit for bit in range(bits) if bit != pair]
    spots = []
    for n in range(size):
        spot = (n & 1) << (bits - 1 - pair)
        for i, bit in enumerate(sums):
            spot |= ((n >> (bits - 1 - i)) & 1) << (bits - 1 - bit)
        spots.append(spot)
    return spots


def local_from_pair(size, pair):
    order = pair_order(size, pair)
    return [order.index(spot) for spot in range(size)]


def project_near(chain, places, scaled, gate, up, pair, area, start, skip, width, req_size):
    rows, depth = scaled.shape
    half, block = rows // 2, rows // req_size
    order = pair_order(req_size, pair)

    def body(places_ref, scaled_ref, gate_ref, up_ref, send_ref, keep_ref):
        mine = lax.rem(places_ref[0] // (1 << pair), 2)
        columns = pl.ds(pl.multiple_of(start + mine * area + skip, 128), width)
        for first, out_ref in ((req_size // 2, send_ref), (0, keep_ref)):
            left = jnp.concatenate(
                [
                    scaled_ref[spot * block : (spot + 1) * block]
                    for spot in order[first : first + req_size // 2]
                ],
                axis=0,
            )
            for i, weight_ref in enumerate((gate_ref, up_ref)):
                out_ref[:, i * width : (i + 1) * width] = jnp.dot(
                    left, weight_ref[:, columns], preferred_element_type=jnp.float32
                ).astype(jnp.bfloat16)

    out = array((half, 2 * width), jnp.bfloat16)
    return chain.run(body, [out, out], [places, scaled, gate, up], [SCALARS, None, None, None])


def project_pair(chain, places, near, squares, far, got, pair, skip, width, req_size):
    half = near[0].shape[0]
    rows = 2 * half
    block = rows // req_size
    depth = far[0].shape[1] - 128
    order = pair_order(req_size, pair)
    flip = 1 << (req_size.bit_length() - 2 - pair)
    cut = got[0].shape[0] - depth
    total = 2 * width + (0 if squares is None else 128)

    def body(places_ref, *refs):
        near_refs, (far_ref, away_ref), (early_ref, late_ref) = refs[:2], refs[2:4], refs[4:6]
        send_ref, keep_ref, all_far = refs[-3:]
        for away, ref in ((0, far_ref), (1, away_ref)):
            first = 1 - places_ref[1] if away else places_ref[1]
            all_far[pl.ds(pl.multiple_of(first * half, half), half)] = ref[...]
        outs = ((order[req_size // 2 :], send_ref), (order[: req_size // 2], keep_ref))

        def take(ref, spots, span, change=0):
            return jnp.concatenate(
                [
                    ref[(spot ^ change) * block : ((spot ^ change) + 1) * block, span]
                    for spot in spots
                ],
                axis=0,
            )

        for near_ref, (spots, out_ref) in zip(near_refs, outs, strict=True):
            for i in range(2):
                spans = [(early_ref, 0, 0, depth)]
                if i == 1:
                    spans = [(early_ref, depth, 0, cut), (late_ref, 0, cut, depth)]
                columns = slice(i * width, (i + 1) * width)
                product = near_ref[:, columns].astype(jnp.float32)
                for ref, top, begin, end in spans:
                    if end > begin:
                        product = product + jnp.dot(
                            take(all_far, spots, slice(begin, end), flip),
                            ref[top : top + end - begin, skip : skip + width],
                            preferred_element_type=jnp.float32,
                        )
                out_ref[:, columns] = product.astype(jnp.bfloat16)
            if squares is not None:
                out_ref[:, 2 * width :] = (
                    take(refs[6], spots, slice(0, 128))
                    + take(all_far, spots, slice(depth, depth + 128), flip).astype(jnp.float32)
                ).astype(jnp.bfloat16)

    ins = [places, *near, *far, *got] + ([] if squares is None else [squares])
    out = array((half, total), jnp.bfloat16)
    return chain.run(
        body,
        [out, out],
        ins,
        [SCALARS] + [None] * (len(ins) - 1),
        scratch=[pltpu.VMEM((rows, depth + 128), jnp.bfloat16)],
    )


def add_halve(chain, other, kept):
    half = kept.shape[0] // 2

    def body(other_ref, kept_ref, send_ref, keep_ref):
        for start, out_ref in ((half, send_ref), (0, keep_ref)):
            rows = slice(start, start + half)
            out_ref[...] = (
                other_ref[rows].astype(jnp.float32) + kept_ref[rows].astype(jnp.float32)
            ).astype(jnp.bfloat16)

    out = array((half, kept.shape[1]), jnp.bfloat16)
    return chain.run(body, [out, out], [other, kept])


def activate(chain, other, kept, inverse, width):
    rows = kept.shape[0]
    first = inverse is None

    def body(other_ref, kept_ref, *refs):
        def total(columns):
            return other_ref[:, columns].astype(jnp.float32) + kept_ref[:, columns].astype(
                jnp.float32
            )

        if first:
            hidden_ref, inverse_ref = refs
            scale = 1.0 / jnp.sqrt(total(slice(2 * width, 2 * width + 128)) / MODEL_WIDTH + EPS)
            inverse_ref[...] = scale
        else:
            scale_ref, hidden_ref = refs
            scale = scale_ref[:rows]
        scale = scale[:, :1]
        gate = total(slice(0, width)) * scale
        up = total(slice(width, 2 * width)) * scale
        hidden_ref[...] = (gate / (1.0 + jnp.exp(-gate)) * up).astype(jnp.bfloat16)

    outs = [array((rows, width), jnp.bfloat16)]
    ins = [other, kept]
    if first:
        outs.append(array((rows, 128), jnp.float32))
    else:
        ins.append(inverse)
    results = chain.run(body, outs, ins)
    return results if first else (results[0], inverse)


def join(chain, kept, other, after=()):
    rows = kept.shape[0]

    def body(kept_ref, other_ref, out_ref):
        out_ref[:rows] = kept_ref[...]
        out_ref[rows:] = other_ref[...]

    return chain.run(
        body, [array((2 * rows, kept.shape[1]), kept.dtype)], [kept, other], after=after
    )[0]


def lower(chain, places, kept, other, down, pair, area, start, skip, width, carried, req_size):
    columns = down.shape[1]
    paired = pair is not None
    rows = kept.shape[0] * (1 if paired else 2)
    half, block = rows // 2, rows // req_size
    back = local_from_pair(req_size, pair) if paired else None

    def body(places_ref, kept_ref, other_ref, down_ref, *refs):
        out_ref = refs[-1]

        def product(left, first):
            return jnp.dot(
                left, down_ref[pl.ds(first, width)], preferred_element_type=jnp.float32
            )

        def take(ref, flip):
            return jnp.concatenate(
                [ref[(n ^ flip) * block : ((n ^ flip) + 1) * block] for n in back], axis=0
            )

        if paired:
            mine = lax.rem(places_ref[0] // (1 << pair), 2)
            total = product(take(kept_ref, 0), pl.multiple_of(start + mine * area + skip, 128))
            total = total + product(
                take(other_ref, 1), pl.multiple_of(start + (1 - mine) * area + skip, 128)
            )
            out_ref[...] = total if carried is None else refs[0][...] + total
        else:
            for first, ref in ((0, kept_ref), (half, other_ref)):
                span = slice(first, first + half)
                total = product(ref[...], start)
                out_ref[span] = total if carried is None else refs[0][span] + total

    ins = [places, kept, other, down] + ([] if carried is None else [carried])
    return chain.run(
        body, [array((rows, columns), jnp.float32)], ins, [SCALARS] + [None] * (len(ins) - 1)
    )[0]


def split_for_kv(chain, total, places, req_size, kv_size):
    rows, columns = total.shape
    bits = req_size.bit_length() - 1
    block = rows // req_size
    per = req_size // kv_size

    def body(places_ref, total_ref, send_ref, keep_ref):
        req_place, mine = places_ref[0], places_ref[1]
        for spot in range(req_size):
            actual = req_place ^ bit_reverse(spot, bits)
            owner = actual // per
            start = pl.multiple_of(((owner // 2) * per + actual % per) * block, block)
            value = total_ref[spot * block : (spot + 1) * block].astype(jnp.bfloat16)

            @pl.when(owner % 2 == mine)
            def _():
                keep_ref[pl.ds(start, block)] = value

            @pl.when(owner % 2 != mine)
            def _():
                send_ref[pl.ds(start, block)] = value

    out = array((rows // 2, columns), jnp.bfloat16)
    return chain.run(
        body,
        [out, out],
        [places, total],
        [SCALARS, None],
    )


class Chunk:
    def __init__(self, pair, start, area, skip, width, bits):
        self.pair, self.start, self.area, self.skip, self.width = pair, start, area, skip, width
        self.sums = [bit for bit in range(bits) if bit != pair]
        self.gathers = [*reversed(self.sums), *([] if pair is None else [pair])]
        self.kept = self.moving = None


def areas_of(columns):
    tiles = columns // 128
    return tiles // 4 * 128, tiles // 4 * 128


def plan(columns, bits):
    first, second = areas_of(columns)
    rest = columns - 2 * first - 2 * second
    chunks = [Chunk(0, 0, first, 0, first, bits), Chunk(1, 2 * first, second, 0, second, bits)]
    if rest:
        chunks.insert(0, Chunk(None, columns - rest, 0, 0, rest, bits))
    stages = 2 * bits + 1
    tasks = [
        (i, stage)
        for stage in range(stages)
        for i, chunk in enumerate(chunks)
        if stage <= len(chunk.sums) + len(chunk.gathers)
    ]
    return chunks, tasks


def feed_forward(chain, places, scaled, squares, far_parts, gots, gate, up, down, req_size, kv_size):
    bits = req_size.bit_length() - 1
    total = None
    inverses = {}
    chunks, tasks = plan(gate.shape[1], bits)
    nears = [
        project_near(
            chain, places, scaled, gate, up, c.pair, c.area, c.start, c.skip, c.width, req_size
        )
        if c.pair is not None
        else None
        for c in chunks
    ]
    fars = [relay(chain, v) for v in far_parts]
    fars = [(v, kv_exchange(v, kv_size, 0)) for v in fars]
    for i, stage in tasks:
        chunk = chunks[i]
        pair, sums, gathers = chunk.pair, chunk.sums, chunk.gathers
        if stage == 0:
            if pair is not None:
                send, chunk.kept = project_pair(
                    chain,
                    places,
                    nears[i],
                    squares if chunk.skip == 0 else None,
                    fars[pair],
                    gots[pair],
                    pair,
                    chunk.skip,
                    chunk.width,
                    req_size,
                )
            else:
                send, chunk.kept = project(
                    chain, scaled, squares, gate, up, chunk.start, chunk.width
                )
            chunk.moving = exchange(send, req_size, sums[0])
        elif stage < len(sums):
            send, chunk.kept = add_halve(chain, chunk.moving, chunk.kept)
            chunk.moving = exchange(send, req_size, sums[stage])
        elif stage == len(sums):
            chunk.kept, inverses[pair] = activate(
                chain,
                chunk.moving,
                chunk.kept,
                inverses.get(pair),
                chunk.width,
            )
            chunk.moving = exchange(chunk.kept, req_size, gathers[0])
        elif stage < len(sums) + len(gathers):
            chunk.kept = join(chain, chunk.kept, chunk.moving)
            chunk.moving = exchange(chunk.kept, req_size, gathers[stage - len(sums)])
        else:
            total = lower(
                chain,
                places,
                chunk.kept,
                chunk.moving,
                down,
                pair,
                chunk.area,
                chunk.start,
                chunk.skip,
                chunk.width,
                total,
                req_size,
            )
    return total


def shards(
    residual_in,
    attn_gain,
    query_weight,
    key_matrix,
    value_matrix,
    key_cache,
    cached_values,
    cache_lengths,
    positions,
    output_weight,
    mlp_gain,
    gate_weight,
    up_weight,
    down_weight,
):
    req_size = lax.axis_size("req")
    kv_size = lax.axis_size("kv")
    req_place = lax.axis_index("req")
    kv_place = lax.axis_index("kv")
    local_rows = residual_in.shape[0] // req_size
    heads_here, head_size = key_cache.shape[1], key_cache.shape[3]
    tokens = lax.all_to_all(
        residual_in.reshape(req_size, local_rows, -1), "req", split_axis=0, concat_axis=0
    )
    features = query_weight.shape[1]
    places = jnp.stack([req_place, lax.rem(kv_place, 2), kv_place]).astype(jnp.int32)
    areas = areas_of(gate_weight.shape[1])
    theirs = []
    for pair, area in enumerate(areas):
        first = 2 * sum(areas[:pair]) + (1 - lax.rem(req_place // (1 << pair), 2)) * area
        slices = [lax.dynamic_slice_in_dim(v, first, area, 1) for v in (gate_weight, up_weight)]
        cut = EARLY_ROWS[pair] * gate_weight.shape[0] // 512
        early = jnp.concatenate([slices[0], slices[1][:cut]], axis=0) if cut else slices[0]
        theirs.append((early, slices[1][cut:]))
    start = corner(tokens)
    gots = [
        [exchange(tie(theirs[0][0], start, theirs[0][1], *theirs[1]), req_size, 0)],
        [exchange(tie(theirs[1][0], start), req_size, 1)],
    ]
    attended_rows = attention(
        tokens,
        attn_gain,
        (query_weight, key_matrix, value_matrix),
        (key_cache, cached_values),
        rotary_tables(positions, head_size),
        cache_lengths,
        heads_here,
        head_size,
    )
    chain = Chain(attended_rows)
    output_rows, residual_rows = fetch(
        chain, places, features, output_weight, residual_in, req_size
    )
    gathered = attended_rows
    bits = req_size.bit_length() - 1
    for bit in reversed(range(bits)):
        other = exchange(gathered, req_size, bit)
        early = {bits - 1: [gots[1][0]], 0: [gots[0][0]]}.get(bit, [])
        gathered = join(chain, gathered, other, early)
        if bit < 2:
            late = tie(theirs[bit][1], corner(gathered))
            gots[bit].append(exchange(late, req_size, bit))
    partial_mix = mix(chain, gathered, output_rows)
    gain = mlp_gain.reshape(1, -1)
    send, part = half_sum(chain, places, partial_mix, kv_exchange(partial_mix, kv_size, 0))
    for bit in range(1, kv_size.bit_length() - 1):
        send, part = next_sum(chain, part, kv_exchange(send, kv_size, bit))
    beside = kv_exchange(send, kv_size, 0)
    near_part = middle_half(chain, places, send, residual_rows, gain)
    far_parts = [exchange(near_part, req_size, pair) for pair in range(2)]
    scaled, middle, squares = middle_rows(chain, places, send, beside, residual_rows, gain)
    gate, up, down = gate_weight, up_weight, down_weight
    total = feed_forward(
        chain, places, scaled, squares, far_parts, gots, gate, up, down, req_size, kv_size
    )
    send, kept = split_for_kv(chain, total, places, req_size, kv_size)
    value = kept.astype(jnp.float32) + kv_exchange(send, kv_size, 0).astype(jnp.float32)
    for bit in reversed(range(1, kv_size.bit_length() - 1)):
        half = value.shape[0] // 2
        mine = lax.rem(kv_place >> bit, 2)
        other = kv_exchange(
            lax.dynamic_slice_in_dim(value, (1 - mine) * half, half, 0).astype(jnp.bfloat16),
            kv_size,
            bit,
        )
        value = lax.dynamic_slice_in_dim(value, mine * half, half, 0) + other.astype(jnp.float32)
    per = req_size // kv_size
    base_rows = jnp.concatenate(
        [
            lax.dynamic_slice_in_dim(
                middle,
                local_spot(req_place, kv_place * per + i, req_size) * local_rows,
                local_rows,
                0,
            )
            for i in range(per)
        ],
        axis=0,
    )
    return (base_rows + value).astype(jnp.bfloat16)


def solution(mesh):
    return jax.shard_map(
        shards,
        mesh=mesh,
        in_specs=(
            P(None, "req"),
            P(),
            P(None, "kv"),
            P(None, "kv"),
            P(None, "kv"),
            P("req", "kv", None, None),
            P("req", "kv", None, None),
            P("req"),
            P("req"),
            P(None, "req"),
            P("req"),
            P("req", "kv"),
            P("req", "kv"),
            P("kv", "req"),
        ),
        out_specs=P("kv", "req"),
        check_vma=False,
    )
```

```python
import math

import jax
import jax.numpy as jnp
from jax import lax
from jax.experimental import pallas as pl
from jax.experimental.pallas import tpu as pltpu
from jax.sharding import PartitionSpec as P

MODEL_WIDTH = 4096
WINDOW = 512
SINKS = 4


EPS = 1e-05
THETA = 10000.0
JOINED = 4
SPLIT = 2
FETCH_VMEM = 32
EARLY_ROWS = (256, 0)
PRELOAD_VMEM = 40 * 1024 * 1024
ATTENTION_VMEM = 32 * 1024 * 1024


def rotary_tables(places, head_size):
    half = head_size // 2
    freqs = jnp.exp(jnp.arange(half, dtype=jnp.float32) * (-2.0 * math.log(THETA) / head_size))
    angles = places.astype(jnp.float32)[:, None] * freqs[None, :]
    cosine, sine = jnp.cos(angles), jnp.sin(angles)
    return jnp.concatenate([cosine, cosine], axis=1), jnp.concatenate([-sine, sine], axis=1)


def attention(tokens, gain, weights, caches, tables, limits, heads_here, head_size):
    pieces, rows, depth = tokens.shape
    query_weight, key_matrix, value_matrix = weights
    keys, values = caches
    slots = keys.shape[2]
    heads = query_weight.shape[1] // head_size
    query_group = heads // heads_here
    members = min(rows, max(1, 128 // heads))
    lanes = members * heads
    factor = 1.0 / math.sqrt(head_size)

    def body(
        tokens_ref,
        gain_ref,
        query_ref,
        key_ref,
        value_ref,
        keys_far,
        values_far,
        cosine_ref,
        sine_ref,
        limits_ref,
        out_ref,
        flat_ref,
        query_rows,
        key_rows,
        value_rows,
        mixed_rows,
        keys_ref,
        values_ref,
        cache_sems,
    ):
        def cache_copy(group, which):
            far, near = ((keys_far, keys_ref), (values_far, values_ref))[which]
            span = pl.ds(group * members, members)
            return pltpu.make_async_copy(far.at[span], near.at[span], cache_sems.at[group, which])

        for which in range(2):
            for group in range(rows // members):
                cache_copy(group, which).start()
        squares = jnp.zeros((rows, 1), jnp.float32)
        for piece in range(pieces):
            part = tokens_ref[piece].astype(jnp.float32)
            squares = squares + jnp.sum(part * part, axis=1, keepdims=True)
        scale = 1.0 / jnp.sqrt(squares / MODEL_WIDTH + EPS)
        sums = [None, None, None]
        for piece in range(pieces):
            span = slice(piece * depth, (piece + 1) * depth)
            part = tokens_ref[piece].astype(jnp.float32)
            normed = (part * scale * gain_ref[:, span]).astype(jnp.bfloat16)
            for i, weight_ref in enumerate((query_ref, key_ref, value_ref)):
                product = jnp.dot(normed, weight_ref[span], preferred_element_type=jnp.float32)
                sums[i] = product if sums[i] is None else sums[i] + product
        cosine, sine = cosine_ref[...], sine_ref[...]

        def turned(value):
            swapped = jnp.concatenate(
                [value[:, head_size // 2 :], value[:, : head_size // 2]], axis=1
            )
            return (value * cosine + swapped * sine).astype(jnp.bfloat16).astype(jnp.float32)

        def put(ref, head, value):
            for group in range(rows // members):
                ref[pl.ds(group * lanes + head, members, stride=heads), :] = value[
                    group * members : (group + 1) * members
                ]

        for head in range(heads):
            own = head // query_group
            put(query_rows, head, turned(sums[0][:, head * head_size : (head + 1) * head_size]))
            if head % query_group == 0:
                new_key = turned(sums[1][:, own * head_size : (own + 1) * head_size])
                new_value = sums[2][:, own * head_size : (own + 1) * head_size]
                new_value = new_value.astype(jnp.bfloat16).astype(jnp.float32)
            put(key_rows, head, new_key)
            put(value_rows, head, new_value)
        slot = lax.broadcasted_iota(jnp.int32, (slots, lanes), 0)
        owner = lax.broadcasted_iota(jnp.int32, (head_size, lanes), 1) // query_group
        kept = []
        for group in range(rows // members):
            mine = slice(group * lanes, (group + 1) * lanes)
            query_columns = query_rows[mine].T
            own_score = (
                jnp.sum(query_columns * key_rows[mine].T, axis=0, keepdims=True) * factor
            )
            narrow = query_columns.astype(jnp.bfloat16)
            cache_copy(group, 0).wait()
            cut = slots // SPLIT
            parts = [None] * SPLIT
            for first in range(0, members, JOINED):
                pairs = [
                    (member, g)
                    for member in range(first, min(first + JOINED, members))
                    for g in range(heads_here)
                ]
                right = jnp.concatenate(
                    [
                        jnp.where(owner == member * heads_here + g, narrow, jnp.zeros_like(narrow))
                        for member, g in pairs
                    ],
                    axis=0,
                )
                for i in range(SPLIT):
                    left = jnp.concatenate(
                        [
                            keys_ref[group * members + member, g, i * cut : (i + 1) * cut]
                            for member, g in pairs
                        ],
                        axis=1,
                    )
                    product = jnp.dot(left, right, preferred_element_type=jnp.float32)
                    parts[i] = product if parts[i] is None else parts[i] + product
            scores = jnp.concatenate(parts, axis=0)
            lane_member = lax.broadcasted_iota(jnp.int32, (1, lanes), 1) // heads
            limit = jnp.zeros((1, lanes), jnp.int32)
            for member in range(members):
                limit = jnp.where(lane_member == member, limits_ref[group * members + member], limit)
            allowed = (slot < limit) & ((slot < SINKS) | (slot > limit - WINDOW))
            scores = jnp.where(allowed, scores * factor, -1e30)
            peak = jnp.maximum(jnp.max(scores, axis=0, keepdims=True), own_score)
            expo = jnp.where(allowed, jnp.exp(scores - peak), 0.0)
            own_expo = jnp.exp(own_score - peak)
            inverse = 1.0 / (jnp.sum(expo, axis=0, keepdims=True) + own_expo)
            shares = (expo * inverse).T
            own_share = (own_expo * inverse).astype(jnp.bfloat16).astype(jnp.float32)
            own_part = (
                jnp.broadcast_to(own_share, (head_size, lanes)).T * value_rows[mine]
            )
            kept.append((shares, own_part))
        for group, (shares, own_part) in enumerate(kept):
            cache_copy(group, 1).wait()
            for member in range(members):
                request = group * members + member
                span = slice(member * heads, (member + 1) * heads)
                wide = jnp.dot(
                    shares[span].astype(jnp.bfloat16),
                    jnp.concatenate([values_ref[request, g] for g in range(heads_here)], axis=1),
                    preferred_element_type=jnp.float32,
                )
                which = lax.broadcasted_iota(jnp.int32, (heads, head_size), 0) // query_group
                mixed = wide[:, :head_size]
                for g in range(1, heads_here):
                    mixed = jnp.where(which == g, wide[:, g * head_size : (g + 1) * head_size], mixed)
                mixed_rows[group * lanes + member * heads : group * lanes + (member + 1) * heads] = (
                    mixed + own_part[span]
                )
        for head in range(heads):
            for group in range(rows // members):
                flat_ref[group * members : (group + 1) * members, :] = mixed_rows[
                    pl.ds(group * lanes + head, members, stride=heads), :
                ]
            out_ref[:, head * head_size : (head + 1) * head_size] = flat_ref[...].astype(
                jnp.bfloat16
            )

    tall = pltpu.VMEM((rows * heads, head_size), jnp.float32)
    near = pl.BlockSpec(memory_space=pltpu.VMEM)
    return pl.pallas_call(
        body,
        out_shape=array((rows, heads * head_size), jnp.bfloat16),
        in_specs=[*[near] * 5, HBM, HBM, near, near, SCALARS],
        out_specs=pl.BlockSpec(memory_space=pltpu.VMEM),
        scratch_shapes=[
            pltpu.VMEM((rows, head_size), jnp.float32),
            *[tall] * 4,
            *[pltpu.VMEM(v.shape, v.dtype) for v in caches],
            pltpu.SemaphoreType.DMA((rows // members, 2)),
        ],
        compiler_params=pltpu.CompilerParams(vmem_limit_bytes=ATTENTION_VMEM),
    )(
        tokens,
        gain.reshape(1, -1),
        *weights,
        *caches,
        *tables,
        limits,
    )


def bit_reverse(value, bits):
    result = 0
    for bit in range(bits):
        result |= ((value >> bit) & 1) << (bits - 1 - bit)
    return result


def exchange(value, size, bit):
    return lax.ppermute(value, "req", [(i, i ^ (1 << bit)) for i in range(size)])


def local_spot(place, block, size):
    bits = size.bit_length() - 1
    other = place ^ block
    spot = jnp.int32(0)
    for bit in range(bits):
        spot = spot | (((other >> bit) & 1) << (bits - 1 - bit))
    return spot


def kv_exchange(value, size, bit):
    return lax.ppermute(value, "kv", [(i, i ^ (1 << bit)) for i in range(size)])


class Chain:
    def __init__(self, token):
        self.token = token

    def run(self, body, outs, ins, in_specs=None, after=(), scratch=(), vmem=32, cost=0):
        specs = list(in_specs or [None] * len(ins))
        specs = [pl.BlockSpec(memory_space=pltpu.VMEM) if v is None else v for v in specs]
        count = len(ins)
        unread = [self.token, *after]

        def kernel(*refs):
            body(*refs[:count], *refs[count + len(unread) :])

        results = pl.pallas_call(
            kernel,
            out_shape=outs,
            in_specs=[*specs, *[pl.BlockSpec(memory_space=pl.ANY)] * len(unread)],
            out_specs=[pl.BlockSpec(memory_space=pltpu.VMEM)] * len(outs),
            scratch_shapes=scratch,
            compiler_params=pltpu.CompilerParams(vmem_limit_bytes=vmem * 1024 * 1024),
            cost_estimate=pl.CostEstimate(flops=0, bytes_accessed=cost, transcendentals=0),
        )(*ins, *unread)
        self.token = results[0]
        return results


SCALARS = pl.BlockSpec(memory_space=pltpu.SMEM)
FAR = pl.BlockSpec(memory_space=pl.ANY)
HBM = pl.BlockSpec(memory_space=pltpu.HBM)


def array(shape, dtype):
    return jax.ShapeDtypeStruct(shape, dtype)


def corner(value):
    return value.reshape(-1, value.shape[-1])[:16, :128]


def tie(value, *after):
    def body(*refs):
        del refs

    return pl.pallas_call(
        body,
        out_shape=array(value.shape, value.dtype),
        in_specs=[FAR] * (1 + len(after)),
        out_specs=FAR,
        input_output_aliases={0: 0},
        cost_estimate=pl.CostEstimate(flops=0, bytes_accessed=0, transcendentals=0),
    )(value, *after)


def fetch(chain, places, features, output_weight, residual_in, req_size):
    total, columns = residual_in.shape
    bits = req_size.bit_length() - 1
    block = total // req_size

    def body(places_ref, weight_far, residual_ref, weight_ref, ordered_ref, sem):
        start = pl.multiple_of(places_ref[2] * features, features)
        copy = pltpu.make_async_copy(weight_far.at[pl.ds(start, features)], weight_ref, sem)
        copy.start()
        for spot in range(req_size):
            first = pl.multiple_of((places_ref[0] ^ bit_reverse(spot, bits)) * block, block)
            ordered_ref[spot * block : (spot + 1) * block] = residual_ref[pl.ds(first, block)]
        copy.wait()

    return chain.run(
        body,
        [
            array((features, columns), output_weight.dtype),
            array(residual_in.shape, residual_in.dtype),
        ],
        [places, output_weight, residual_in],
        [SCALARS, HBM, None],
        scratch=[pltpu.SemaphoreType.DMA(())],
        vmem=FETCH_VMEM,
    )


def mix(chain, rows, weight):
    def body(rows_ref, weight_ref, out_ref):
        out_ref[...] = jnp.dot(
            rows_ref[...], weight_ref[...], preferred_element_type=jnp.float32
        ).astype(jnp.bfloat16)

    out = array((rows.shape[0], weight.shape[1]), jnp.bfloat16)
    return chain.run(body, [out], [rows, weight])[0]


def half_sum(chain, places, rows, other):
    half, columns = rows.shape[0] // 2, rows.shape[1]

    def body(places_ref, rows_ref, other_ref, send_ref, part_ref):
        span = pl.ds(pl.multiple_of(places_ref[1] * half, half), half)
        part = rows_ref[span].astype(jnp.float32) + other_ref[span].astype(jnp.float32)
        part_ref[...] = part
        send_ref[...] = part.astype(jnp.bfloat16)

    return chain.run(
        body,
        [array((half, columns), jnp.bfloat16), array((half, columns), jnp.float32)],
        [places, rows, other],
        [SCALARS, None, None],
    )


def relay(chain, value):
    def body(value_ref, out_ref):
        out_ref[...] = value_ref[...]

    return chain.run(body, [array(value.shape, value.dtype)], [value])[0]


def next_sum(chain, part, other):
    def body(part_ref, other_ref, send_ref, sum_ref):
        total = part_ref[...] + other_ref[...].astype(jnp.float32)
        sum_ref[...] = total
        send_ref[...] = total.astype(jnp.bfloat16)

    return chain.run(
        body, [array(part.shape, jnp.bfloat16), array(part.shape, jnp.float32)], [part, other]
    )


def middle_half(chain, places, mixed, residual_rows, gain):
    half, columns = mixed.shape

    def body(places_ref, mixed_ref, residual_ref, gain_ref, out_ref):
        span = pl.ds(pl.multiple_of(places_ref[1] * half, half), half)
        middle = residual_ref[span].astype(jnp.float32) + mixed_ref[...].astype(jnp.float32)
        out_ref[:, :columns] = (middle * gain_ref[...]).astype(jnp.bfloat16)
        out_ref[:, columns:] = jnp.broadcast_to(
            jnp.sum(middle * middle, axis=1, keepdims=True), (half, 128)
        ).astype(jnp.bfloat16)

    return chain.run(
        body,
        [array((half, columns + 128), jnp.bfloat16)],
        [places, mixed, residual_rows, gain],
        [SCALARS, None, None, None],
    )[0]


def middle_rows(chain, places, mixed, other, residual_rows, gain):
    half, columns = mixed.shape
    rows = 2 * half

    def body(places_ref, mixed_ref, other_ref, residual_ref, gain_ref, scaled_ref, middle_ref, squares_ref):
        for mine, ref in ((0, mixed_ref), (1, other_ref)):
            first = places_ref[1] if mine == 0 else 1 - places_ref[1]
            span = pl.ds(pl.multiple_of(first * half, half), half)
            middle = residual_ref[span].astype(jnp.float32) + ref[...].astype(jnp.float32)
            middle_ref[span] = middle
            scaled_ref[span] = (middle * gain_ref[...]).astype(jnp.bfloat16)
            squares_ref[span] = jnp.broadcast_to(
                jnp.sum(middle * middle, axis=1, keepdims=True), (half, 128)
            )

    return chain.run(
        body,
        [
            array((rows, columns), jnp.bfloat16),
            array((rows, columns), jnp.float32),
            array((rows, 128), jnp.float32),
        ],
        [places, mixed, other, residual_rows, gain],
        [SCALARS, None, None, None, None],
    )


def project(chain, scaled, squares, gate, up, start, width):
    half = scaled.shape[0] // 2

    def body(scaled_ref, gate_ref, up_ref, squares_ref, send_ref, keep_ref):
        for first, out_ref in ((half, send_ref), (0, keep_ref)):
            left = scaled_ref[first : first + half]
            for i, weight_ref in enumerate((gate_ref, up_ref)):
                out_ref[:, i * width : (i + 1) * width] = jnp.dot(
                    left, weight_ref[:, start : start + width], preferred_element_type=jnp.float32
                ).astype(jnp.bfloat16)

            out_ref[:, 2 * width :] = squares_ref[first : first + half].astype(jnp.bfloat16)

    out = array((half, 2 * width + 128), jnp.bfloat16)
    return chain.run(body, [out, out], [scaled, gate, up, squares])


def pair_order(size, pair):
    bits = size.bit_length() - 1
    sums = [bit for bit in range(bits) if bit != pair]
    spots = []
    for n in range(size):
        spot = (n & 1) << (bits - 1 - pair)
        for i, bit in enumerate(sums):
            spot |= ((n >> (bits - 1 - i)) & 1) << (bits - 1 - bit)
        spots.append(spot)
    return spots


def local_from_pair(size, pair):
    order = pair_order(size, pair)
    return [order.index(spot) for spot in range(size)]


def project_near(chain, places, scaled, gate, up, pair, area, start, skip, width, req_size):
    rows, depth = scaled.shape
    half, block = rows // 2, rows // req_size
    order = pair_order(req_size, pair)

    def body(places_ref, scaled_ref, gate_ref, up_ref, send_ref, keep_ref):
        mine = lax.rem(places_ref[0] // (1 << pair), 2)
        columns = pl.ds(pl.multiple_of(start + mine * area + skip, 128), width)
        for first, out_ref in ((req_size // 2, send_ref), (0, keep_ref)):
            left = jnp.concatenate(
                [
                    scaled_ref[spot * block : (spot + 1) * block]
                    for spot in order[first : first + req_size // 2]
                ],
                axis=0,
            )
            for i, weight_ref in enumerate((gate_ref, up_ref)):
                out_ref[:, i * width : (i + 1) * width] = jnp.dot(
                    left, weight_ref[:, columns], preferred_element_type=jnp.float32
                ).astype(jnp.bfloat16)

    out = array((half, 2 * width), jnp.bfloat16)
    return chain.run(body, [out, out], [places, scaled, gate, up], [SCALARS, None, None, None])


def project_pair(chain, places, near, squares, far, got, pair, skip, width, req_size):
    half = near[0].shape[0]
    rows = 2 * half
    block = rows // req_size
    depth = far[0].shape[1] - 128
    order = pair_order(req_size, pair)
    flip = 1 << (req_size.bit_length() - 2 - pair)
    cut = got[0].shape[0] - depth
    total = 2 * width + (0 if squares is None else 128)

    def body(places_ref, *refs):
        near_refs, (far_ref, away_ref), (early_ref, late_ref) = refs[:2], refs[2:4], refs[4:6]
        send_ref, keep_ref, all_far = refs[-3:]
        for away, ref in ((0, far_ref), (1, away_ref)):
            first = 1 - places_ref[1] if away else places_ref[1]
            all_far[pl.ds(pl.multiple_of(first * half, half), half)] = ref[...]
        outs = ((order[req_size // 2 :], send_ref), (order[: req_size // 2], keep_ref))

        def take(ref, spots, span, change=0):
            return jnp.concatenate(
                [
                    ref[(spot ^ change) * block : ((spot ^ change) + 1) * block, span]
                    for spot in spots
                ],
                axis=0,
            )

        for near_ref, (spots, out_ref) in zip(near_refs, outs, strict=True):
            for i in range(2):
                spans = [(early_ref, 0, 0, depth)]
                if i == 1:
                    spans = [(early_ref, depth, 0, cut), (late_ref, 0, cut, depth)]
                columns = slice(i * width, (i + 1) * width)
                product = near_ref[:, columns].astype(jnp.float32)
                for ref, top, begin, end in spans:
                    if end > begin:
                        product = product + jnp.dot(
                            take(all_far, spots, slice(begin, end), flip),
                            ref[top : top + end - begin, skip : skip + width],
                            preferred_element_type=jnp.float32,
                        )
                out_ref[:, columns] = product.astype(jnp.bfloat16)
            if squares is not None:
                out_ref[:, 2 * width :] = (
                    take(refs[6], spots, slice(0, 128))
                    + take(all_far, spots, slice(depth, depth + 128), flip).astype(jnp.float32)
                ).astype(jnp.bfloat16)

    ins = [places, *near, *far, *got] + ([] if squares is None else [squares])
    out = array((half, total), jnp.bfloat16)
    return chain.run(
        body,
        [out, out],
        ins,
        [SCALARS] + [None] * (len(ins) - 1),
        scratch=[pltpu.VMEM((rows, depth + 128), jnp.bfloat16)],
    )


def add_halve(chain, other, kept):
    half = kept.shape[0] // 2

    def body(other_ref, kept_ref, send_ref, keep_ref):
        for start, out_ref in ((half, send_ref), (0, keep_ref)):
            rows = slice(start, start + half)
            out_ref[...] = (
                other_ref[rows].astype(jnp.float32) + kept_ref[rows].astype(jnp.float32)
            ).astype(jnp.bfloat16)

    out = array((half, kept.shape[1]), jnp.bfloat16)
    return chain.run(body, [out, out], [other, kept])


def activate(chain, other, kept, inverse, width):
    rows = kept.shape[0]
    first = inverse is None

    def body(other_ref, kept_ref, *refs):
        def total(columns):
            return other_ref[:, columns].astype(jnp.float32) + kept_ref[:, columns].astype(
                jnp.float32
            )

        if first:
            hidden_ref, inverse_ref = refs
            scale = 1.0 / jnp.sqrt(total(slice(2 * width, 2 * width + 128)) / MODEL_WIDTH + EPS)
            inverse_ref[...] = scale
        else:
            scale_ref, hidden_ref = refs
            scale = scale_ref[:rows]
        scale = scale[:, :1]
        gate = total(slice(0, width)) * scale
        up = total(slice(width, 2 * width)) * scale
        hidden_ref[...] = (gate / (1.0 + jnp.exp(-gate)) * up).astype(jnp.bfloat16)

    outs = [array((rows, width), jnp.bfloat16)]
    ins = [other, kept]
    if first:
        outs.append(array((rows, 128), jnp.float32))
    else:
        ins.append(inverse)
    results = chain.run(body, outs, ins)
    return results if first else (results[0], inverse)


def join(chain, kept, other, after=()):
    rows = kept.shape[0]

    def body(kept_ref, other_ref, out_ref):
        out_ref[:rows] = kept_ref[...]
        out_ref[rows:] = other_ref[...]

    return chain.run(
        body, [array((2 * rows, kept.shape[1]), kept.dtype)], [kept, other], after=after
    )[0]


def lower(chain, places, kept, other, down, pair, area, start, skip, width, carried, req_size):
    columns = down.shape[1]
    paired = pair is not None
    rows = kept.shape[0] * (1 if paired else 2)
    half, block = rows // 2, rows // req_size
    back = local_from_pair(req_size, pair) if paired else None

    def body(places_ref, kept_ref, other_ref, down_ref, *refs):
        out_ref = refs[-1]

        def product(left, first):
            return jnp.dot(
                left, down_ref[pl.ds(first, width)], preferred_element_type=jnp.float32
            )

        def take(ref, flip):
            return jnp.concatenate(
                [ref[(n ^ flip) * block : ((n ^ flip) + 1) * block] for n in back], axis=0
            )

        if paired:
            mine = lax.rem(places_ref[0] // (1 << pair), 2)
            total = product(take(kept_ref, 0), pl.multiple_of(start + mine * area + skip, 128))
            total = total + product(
                take(other_ref, 1), pl.multiple_of(start + (1 - mine) * area + skip, 128)
            )
            out_ref[...] = total if carried is None else refs[0][...] + total
        else:
            for first, ref in ((0, kept_ref), (half, other_ref)):
                span = slice(first, first + half)
                total = product(ref[...], start)
                out_ref[span] = total if carried is None else refs[0][span] + total

    ins = [places, kept, other, down] + ([] if carried is None else [carried])
    return chain.run(
        body, [array((rows, columns), jnp.float32)], ins, [SCALARS] + [None] * (len(ins) - 1)
    )[0]


def split_for_kv(chain, total, places, req_size, kv_size):
    rows, columns = total.shape
    bits = req_size.bit_length() - 1
    block = rows // req_size
    per = req_size // kv_size

    def body(places_ref, total_ref, send_ref, keep_ref):
        req_place, mine = places_ref[0], places_ref[1]
        for spot in range(req_size):
            actual = req_place ^ bit_reverse(spot, bits)
            owner = actual // per
            start = pl.multiple_of(((owner // 2) * per + actual % per) * block, block)
            value = total_ref[spot * block : (spot + 1) * block].astype(jnp.bfloat16)

            @pl.when(owner % 2 == mine)
            def _():
                keep_ref[pl.ds(start, block)] = value

            @pl.when(owner % 2 != mine)
            def _():
                send_ref[pl.ds(start, block)] = value

    out = array((rows // 2, columns), jnp.bfloat16)
    return chain.run(
        body,
        [out, out],
        [places, total],
        [SCALARS, None],
    )


def lower_half(chain, places, hidden, away, down, pair, area, start, skip, width, carried, req_size):
    rows, columns = hidden.shape[0], down.shape[1]
    block = rows // req_size
    back = local_from_pair(req_size, pair)

    def body(places_ref, hidden_ref, down_ref, *refs):
        mine = lax.rem(places_ref[0] // (1 << pair), 2)
        which = 1 - mine if away else mine
        left = jnp.concatenate(
            [hidden_ref[(n ^ away) * block : ((n ^ away) + 1) * block] for n in back], axis=0
        )
        first = pl.multiple_of(start + which * area + skip, 128)
        total = jnp.dot(left, down_ref[pl.ds(first, width)], preferred_element_type=jnp.float32)
        refs[-1][...] = total if carried is None else refs[0][...] + total

    ins = [places, hidden, down] + ([] if carried is None else [carried])
    return chain.run(
        body, [array((rows, columns), jnp.float32)], ins, [SCALARS] + [None] * (len(ins) - 1)
    )[0]


class Chunk:
    def __init__(self, pair, start, area, skip, width, bits):
        self.pair, self.start, self.area, self.skip, self.width = pair, start, area, skip, width
        self.sums = [bit for bit in range(bits) if bit != pair]
        self.gathers = [*reversed(self.sums), *([] if pair is None else [pair])]
        self.kept = self.moving = None


def areas_of(columns):
    tiles = columns // 128
    return tiles // 4 * 128, tiles // 4 * 128


def plan(columns, bits):
    first, second = areas_of(columns)
    rest = columns - 2 * first - 2 * second
    chunks = [Chunk(0, 0, first, 0, first, bits), Chunk(1, 2 * first, second, 0, second, bits)]
    if rest:
        chunks.insert(0, Chunk(None, columns - rest, 0, 0, rest, bits))
    stages = 2 * bits + 1
    tasks = [
        (i, stage)
        for stage in range(stages)
        for i, chunk in enumerate(chunks)
        if stage <= len(chunk.sums) + len(chunk.gathers)
    ]
    return chunks, tasks


def feed_forward(chain, places, scaled, squares, far_parts, gots, gate, up, down, req_size, kv_size):
    bits = req_size.bit_length() - 1
    total = None
    inverses = {}
    chunks, tasks = plan(gate.shape[1], bits)
    nears = [
        project_near(
            chain, places, scaled, gate, up, c.pair, c.area, c.start, c.skip, c.width, req_size
        )
        if c.pair is not None
        else None
        for c in chunks
    ]
    fars = [relay(chain, v) for v in far_parts]
    fars = [(v, kv_exchange(v, kv_size, 0)) for v in fars]
    for i, stage in tasks:
        chunk = chunks[i]
        pair, sums, gathers = chunk.pair, chunk.sums, chunk.gathers
        if stage == 0:
            if pair is not None:
                send, chunk.kept = project_pair(
                    chain,
                    places,
                    nears[i],
                    squares if chunk.skip == 0 else None,
                    fars[pair],
                    gots[pair],
                    pair,
                    chunk.skip,
                    chunk.width,
                    req_size,
                )
            else:
                send, chunk.kept = project(
                    chain, scaled, squares, gate, up, chunk.start, chunk.width
                )
            chunk.moving = exchange(send, req_size, sums[0])
        elif stage < len(sums):
            send, chunk.kept = add_halve(chain, chunk.moving, chunk.kept)
            chunk.moving = exchange(send, req_size, sums[stage])
        elif stage == len(sums):
            chunk.kept, inverses[pair] = activate(
                chain,
                chunk.moving,
                chunk.kept,
                inverses.get(pair),
                chunk.width,
            )
            chunk.moving = exchange(chunk.kept, req_size, gathers[0])
        elif stage < len(sums) + len(gathers):
            chunk.kept = join(chain, chunk.kept, chunk.moving)
            chunk.moving = exchange(chunk.kept, req_size, gathers[stage - len(sums)])
            if pair is not None and stage == len(sums) + len(gathers) - 1:
                total = lower_half(
                    chain,
                    places,
                    chunk.kept,
                    0,
                    down,
                    pair,
                    chunk.area,
                    chunk.start,
                    chunk.skip,
                    chunk.width,
                    total,
                    req_size,
                )
        elif pair is not None:
            total = lower_half(
                chain,
                places,
                chunk.moving,
                1,
                down,
                pair,
                chunk.area,
                chunk.start,
                chunk.skip,
                chunk.width,
                total,
                req_size,
            )
        else:
            total = lower(
                chain,
                places,
                chunk.kept,
                chunk.moving,
                down,
                pair,
                chunk.area,
                chunk.start,
                chunk.skip,
                chunk.width,
                total,
                req_size,
            )
    return total


def shards(
    residual_in,
    attn_gain,
    query_weight,
    key_matrix,
    value_matrix,
    key_cache,
    cached_values,
    cache_lengths,
    positions,
    output_weight,
    mlp_gain,
    gate_weight,
    up_weight,
    down_weight,
):
    req_size = lax.axis_size("req")
    kv_size = lax.axis_size("kv")
    req_place = lax.axis_index("req")
    kv_place = lax.axis_index("kv")
    local_rows = residual_in.shape[0] // req_size
    heads_here, head_size = key_cache.shape[1], key_cache.shape[3]
    tokens = lax.all_to_all(
        residual_in.reshape(req_size, local_rows, -1), "req", split_axis=0, concat_axis=0
    )
    features = query_weight.shape[1]
    places = jnp.stack([req_place, lax.rem(kv_place, 2), kv_place]).astype(jnp.int32)
    areas = areas_of(gate_weight.shape[1])
    theirs = []
    for pair, area in enumerate(areas):
        first = 2 * sum(areas[:pair]) + (1 - lax.rem(req_place // (1 << pair), 2)) * area
        slices = [lax.dynamic_slice_in_dim(v, first, area, 1) for v in (gate_weight, up_weight)]
        cut = EARLY_ROWS[pair] * gate_weight.shape[0] // 512
        early = jnp.concatenate([slices[0], slices[1][:cut]], axis=0) if cut else slices[0]
        theirs.append((early, slices[1][cut:]))
    start = corner(tokens)
    gots = [
        [exchange(tie(theirs[0][0], start, theirs[0][1], *theirs[1]), req_size, 0)],
        [exchange(tie(theirs[1][0], start), req_size, 1)],
    ]
    attended_rows = attention(
        tokens,
        attn_gain,
        (query_weight, key_matrix, value_matrix),
        (key_cache, cached_values),
        rotary_tables(positions, head_size),
        cache_lengths,
        heads_here,
        head_size,
    )
    chain = Chain(attended_rows)
    output_rows, residual_rows = fetch(
        chain, places, features, output_weight, residual_in, req_size
    )
    gathered = attended_rows
    bits = req_size.bit_length() - 1
    for bit in reversed(range(bits)):
        other = exchange(gathered, req_size, bit)
        early = {bits - 1: [gots[1][0]], 0: [gots[0][0]]}.get(bit, [])
        gathered = join(chain, gathered, other, early)
        if bit < 2:
            late = tie(theirs[bit][1], corner(gathered))
            gots[bit].append(exchange(late, req_size, bit))
    partial_mix = mix(chain, gathered, output_rows)
    gain = mlp_gain.reshape(1, -1)
    send, part = half_sum(chain, places, partial_mix, kv_exchange(partial_mix, kv_size, 0))
    for bit in range(1, kv_size.bit_length() - 1):
        send, part = next_sum(chain, part, kv_exchange(send, kv_size, bit))
    beside = kv_exchange(send, kv_size, 0)
    near_part = middle_half(chain, places, send, residual_rows, gain)
    far_parts = [exchange(near_part, req_size, pair) for pair in range(2)]
    scaled, middle, squares = middle_rows(chain, places, send, beside, residual_rows, gain)
    gate, up, down = gate_weight, up_weight, down_weight
    total = feed_forward(
        chain, places, scaled, squares, far_parts, gots, gate, up, down, req_size, kv_size
    )
    send, kept = split_for_kv(chain, total, places, req_size, kv_size)
    value = kept.astype(jnp.float32) + kv_exchange(send, kv_size, 0).astype(jnp.float32)
    for bit in reversed(range(1, kv_size.bit_length() - 1)):
        half = value.shape[0] // 2
        mine = lax.rem(kv_place >> bit, 2)
        other = kv_exchange(
            lax.dynamic_slice_in_dim(value, (1 - mine) * half, half, 0).astype(jnp.bfloat16),
            kv_size,
            bit,
        )
        value = lax.dynamic_slice_in_dim(value, mine * half, half, 0) + other.astype(jnp.float32)
    per = req_size // kv_size
    base_rows = jnp.concatenate(
        [
            lax.dynamic_slice_in_dim(
                middle,
                local_spot(req_place, kv_place * per + i, req_size) * local_rows,
                local_rows,
                0,
            )
            for i in range(per)
        ],
        axis=0,
    )
    return (base_rows + value).astype(jnp.bfloat16)


def solution(mesh):
    return jax.shard_map(
        shards,
        mesh=mesh,
        in_specs=(
            P(None, "req"),
            P(),
            P(None, "kv"),
            P(None, "kv"),
            P(None, "kv"),
            P("req", "kv", None, None),
            P("req", "kv", None, None),
            P("req"),
            P("req"),
            P(None, "req"),
            P("req"),
            P("req", "kv"),
            P("req", "kv"),
            P("kv", "req"),
        ),
        out_specs=P("kv", "req"),
        check_vma=False,
    )
```

```python
import math

import jax
import jax.numpy as jnp
from jax import lax
from jax.experimental import pallas as pl
from jax.experimental.pallas import tpu as pltpu
from jax.sharding import PartitionSpec as P

MODEL_WIDTH = 4096
WINDOW = 512
SINKS = 4


EPS = 1e-05
THETA = 10000.0
JOINED = 4
SPLIT = 2
FETCH_VMEM = 32
EARLY_ROWS = (256, 0)
PRELOAD_VMEM = 40 * 1024 * 1024
ATTENTION_VMEM = 32 * 1024 * 1024


def rotary_tables(places, head_size):
    half = head_size // 2
    freqs = jnp.exp(jnp.arange(half, dtype=jnp.float32) * (-2.0 * math.log(THETA) / head_size))
    angles = places.astype(jnp.float32)[:, None] * freqs[None, :]
    cosine, sine = jnp.cos(angles), jnp.sin(angles)
    return jnp.concatenate([cosine, cosine], axis=1), jnp.concatenate([-sine, sine], axis=1)


def attention(tokens, gain, weights, caches, tables, limits, heads_here, head_size):
    pieces, rows, depth = tokens.shape
    query_weight, key_matrix, value_matrix = weights
    keys, values = caches
    slots = keys.shape[2]
    heads = query_weight.shape[1] // head_size
    query_group = heads // heads_here
    members = min(rows, max(1, 128 // heads))
    lanes = members * heads
    factor = 1.0 / math.sqrt(head_size)

    def body(
        tokens_ref,
        gain_ref,
        query_ref,
        key_ref,
        value_ref,
        keys_far,
        values_far,
        cosine_ref,
        sine_ref,
        limits_ref,
        out_ref,
        flat_ref,
        query_rows,
        key_rows,
        value_rows,
        mixed_rows,
        keys_ref,
        values_ref,
        cache_sems,
    ):
        def cache_copy(group, which):
            far, near = ((keys_far, keys_ref), (values_far, values_ref))[which]
            span = pl.ds(group * members, members)
            return pltpu.make_async_copy(far.at[span], near.at[span], cache_sems.at[group, which])

        for which in range(2):
            for group in range(rows // members):
                cache_copy(group, which).start()
        squares = jnp.zeros((rows, 1), jnp.float32)
        for piece in range(pieces):
            part = tokens_ref[piece].astype(jnp.float32)
            squares = squares + jnp.sum(part * part, axis=1, keepdims=True)
        scale = 1.0 / jnp.sqrt(squares / MODEL_WIDTH + EPS)
        sums = [None, None, None]
        for piece in range(pieces):
            span = slice(piece * depth, (piece + 1) * depth)
            part = tokens_ref[piece].astype(jnp.float32)
            normed = (part * scale * gain_ref[:, span]).astype(jnp.bfloat16)
            for i, weight_ref in enumerate((query_ref, key_ref, value_ref)):
                product = jnp.dot(normed, weight_ref[span], preferred_element_type=jnp.float32)
                sums[i] = product if sums[i] is None else sums[i] + product
        cosine, sine = cosine_ref[...], sine_ref[...]

        def turned(value):
            swapped = jnp.concatenate(
                [value[:, head_size // 2 :], value[:, : head_size // 2]], axis=1
            )
            return (value * cosine + swapped * sine).astype(jnp.bfloat16).astype(jnp.float32)

        def put(ref, head, value):
            for group in range(rows // members):
                ref[pl.ds(group * lanes + head, members, stride=heads), :] = value[
                    group * members : (group + 1) * members
                ]

        for head in range(heads):
            own = head // query_group
            put(query_rows, head, turned(sums[0][:, head * head_size : (head + 1) * head_size]))
            if head % query_group == 0:
                new_key = turned(sums[1][:, own * head_size : (own + 1) * head_size])
                new_value = sums[2][:, own * head_size : (own + 1) * head_size]
                new_value = new_value.astype(jnp.bfloat16).astype(jnp.float32)
            put(key_rows, head, new_key)
            put(value_rows, head, new_value)
        slot = lax.broadcasted_iota(jnp.int32, (slots, lanes), 0)
        owner = lax.broadcasted_iota(jnp.int32, (head_size, lanes), 1) // query_group
        kept = []
        for group in range(rows // members):
            mine = slice(group * lanes, (group + 1) * lanes)
            query_columns = query_rows[mine].T
            own_score = (
                jnp.sum(query_columns * key_rows[mine].T, axis=0, keepdims=True) * factor
            )
            narrow = query_columns.astype(jnp.bfloat16)
            cache_copy(group, 0).wait()
            cut = slots // SPLIT
            parts = [None] * SPLIT
            for first in range(0, members, JOINED):
                pairs = [
                    (member, g)
                    for member in range(first, min(first + JOINED, members))
                    for g in range(heads_here)
                ]
                right = jnp.concatenate(
                    [
                        jnp.where(owner == member * heads_here + g, narrow, jnp.zeros_like(narrow))
                        for member, g in pairs
                    ],
                    axis=0,
                )
                for i in range(SPLIT):
                    left = jnp.concatenate(
                        [
                            keys_ref[group * members + member, g, i * cut : (i + 1) * cut]
                            for member, g in pairs
                        ],
                        axis=1,
                    )
                    product = jnp.dot(left, right, preferred_element_type=jnp.float32)
                    parts[i] = product if parts[i] is None else parts[i] + product
            scores = jnp.concatenate(parts, axis=0)
            lane_member = lax.broadcasted_iota(jnp.int32, (1, lanes), 1) // heads
            limit = jnp.zeros((1, lanes), jnp.int32)
            for member in range(members):
                limit = jnp.where(lane_member == member, limits_ref[group * members + member], limit)
            allowed = (slot < limit) & ((slot < SINKS) | (slot > limit - WINDOW))
            scores = jnp.where(allowed, scores * factor, -1e30)
            peak = jnp.maximum(jnp.max(scores, axis=0, keepdims=True), own_score)
            expo = jnp.where(allowed, jnp.exp(scores - peak), 0.0)
            own_expo = jnp.exp(own_score - peak)
            inverse = 1.0 / (jnp.sum(expo, axis=0, keepdims=True) + own_expo)
            shares = (expo * inverse).T
            own_share = (own_expo * inverse).astype(jnp.bfloat16).astype(jnp.float32)
            own_part = (
                jnp.broadcast_to(own_share, (head_size, lanes)).T * value_rows[mine]
            )
            kept.append((shares, own_part))
        for group, (shares, own_part) in enumerate(kept):
            cache_copy(group, 1).wait()
            for member in range(members):
                request = group * members + member
                span = slice(member * heads, (member + 1) * heads)
                wide = jnp.dot(
                    shares[span].astype(jnp.bfloat16),
                    jnp.concatenate([values_ref[request, g] for g in range(heads_here)], axis=1),
                    preferred_element_type=jnp.float32,
                )
                which = lax.broadcasted_iota(jnp.int32, (heads, head_size), 0) // query_group
                mixed = wide[:, :head_size]
                for g in range(1, heads_here):
                    mixed = jnp.where(which == g, wide[:, g * head_size : (g + 1) * head_size], mixed)
                mixed_rows[group * lanes + member * heads : group * lanes + (member + 1) * heads] = (
                    mixed + own_part[span]
                )
        for head in range(heads):
            for group in range(rows // members):
                flat_ref[group * members : (group + 1) * members, :] = mixed_rows[
                    pl.ds(group * lanes + head, members, stride=heads), :
                ]
            out_ref[:, head * head_size : (head + 1) * head_size] = flat_ref[...].astype(
                jnp.bfloat16
            )

    tall = pltpu.VMEM((rows * heads, head_size), jnp.float32)
    near = pl.BlockSpec(memory_space=pltpu.VMEM)
    return pl.pallas_call(
        body,
        out_shape=array((rows, heads * head_size), jnp.bfloat16),
        in_specs=[*[near] * 5, HBM, HBM, near, near, SCALARS],
        out_specs=pl.BlockSpec(memory_space=pltpu.VMEM),
        scratch_shapes=[
            pltpu.VMEM((rows, head_size), jnp.float32),
            *[tall] * 4,
            *[pltpu.VMEM(v.shape, v.dtype) for v in caches],
            pltpu.SemaphoreType.DMA((rows // members, 2)),
        ],
        compiler_params=pltpu.CompilerParams(vmem_limit_bytes=ATTENTION_VMEM),
    )(
        tokens,
        gain.reshape(1, -1),
        *weights,
        *caches,
        *tables,
        limits,
    )


def bit_reverse(value, bits):
    result = 0
    for bit in range(bits):
        result |= ((value >> bit) & 1) << (bits - 1 - bit)
    return result


def exchange(value, size, bit):
    return lax.ppermute(value, "req", [(i, i ^ (1 << bit)) for i in range(size)])


def local_spot(place, block, size):
    bits = size.bit_length() - 1
    other = place ^ block
    spot = jnp.int32(0)
    for bit in range(bits):
        spot = spot | (((other >> bit) & 1) << (bits - 1 - bit))
    return spot


def kv_exchange(value, size, bit):
    return lax.ppermute(value, "kv", [(i, i ^ (1 << bit)) for i in range(size)])


class Chain:
    def __init__(self, token):
        self.token = token

    def run(self, body, outs, ins, in_specs=None, after=(), scratch=(), vmem=32, cost=0):
        specs = list(in_specs or [None] * len(ins))
        specs = [pl.BlockSpec(memory_space=pltpu.VMEM) if v is None else v for v in specs]
        count = len(ins)
        unread = [self.token, *after]

        def kernel(*refs):
            body(*refs[:count], *refs[count + len(unread) :])

        results = pl.pallas_call(
            kernel,
            out_shape=outs,
            in_specs=[*specs, *[pl.BlockSpec(memory_space=pl.ANY)] * len(unread)],
            out_specs=[pl.BlockSpec(memory_space=pltpu.VMEM)] * len(outs),
            scratch_shapes=scratch,
            compiler_params=pltpu.CompilerParams(vmem_limit_bytes=vmem * 1024 * 1024),
            cost_estimate=pl.CostEstimate(flops=0, bytes_accessed=cost, transcendentals=0),
        )(*ins, *unread)
        self.token = results[0]
        return results


SCALARS = pl.BlockSpec(memory_space=pltpu.SMEM)
FAR = pl.BlockSpec(memory_space=pl.ANY)
HBM = pl.BlockSpec(memory_space=pltpu.HBM)


def array(shape, dtype):
    return jax.ShapeDtypeStruct(shape, dtype)


def corner(value):
    return value.reshape(-1, value.shape[-1])[:16, :128]


def tie(value, *after):
    def body(*refs):
        del refs

    return pl.pallas_call(
        body,
        out_shape=array(value.shape, value.dtype),
        in_specs=[FAR] * (1 + len(after)),
        out_specs=FAR,
        input_output_aliases={0: 0},
        cost_estimate=pl.CostEstimate(flops=0, bytes_accessed=0, transcendentals=0),
    )(value, *after)


def fetch(chain, places, features, output_weight, residual_in, req_size):
    total, columns = residual_in.shape
    bits = req_size.bit_length() - 1
    block = total // req_size

    def body(places_ref, weight_far, residual_ref, weight_ref, ordered_ref, sem):
        start = pl.multiple_of(places_ref[2] * features, features)
        copy = pltpu.make_async_copy(weight_far.at[pl.ds(start, features)], weight_ref, sem)
        copy.start()
        for spot in range(req_size):
            first = pl.multiple_of((places_ref[0] ^ bit_reverse(spot, bits)) * block, block)
            ordered_ref[spot * block : (spot + 1) * block] = residual_ref[pl.ds(first, block)]
        copy.wait()

    return chain.run(
        body,
        [
            array((features, columns), output_weight.dtype),
            array(residual_in.shape, residual_in.dtype),
        ],
        [places, output_weight, residual_in],
        [SCALARS, HBM, None],
        scratch=[pltpu.SemaphoreType.DMA(())],
        vmem=FETCH_VMEM,
    )


def mix(chain, rows, weight):
    def body(rows_ref, weight_ref, out_ref):
        out_ref[...] = jnp.dot(
            rows_ref[...], weight_ref[...], preferred_element_type=jnp.float32
        ).astype(jnp.bfloat16)

    out = array((rows.shape[0], weight.shape[1]), jnp.bfloat16)
    return chain.run(body, [out], [rows, weight])[0]


def half_sum(chain, places, rows, other):
    half, columns = rows.shape[0] // 2, rows.shape[1]

    def body(places_ref, rows_ref, other_ref, send_ref, part_ref):
        span = pl.ds(pl.multiple_of(places_ref[1] * half, half), half)
        part = rows_ref[span].astype(jnp.float32) + other_ref[span].astype(jnp.float32)
        part_ref[...] = part
        send_ref[...] = part.astype(jnp.bfloat16)

    return chain.run(
        body,
        [array((half, columns), jnp.bfloat16), array((half, columns), jnp.float32)],
        [places, rows, other],
        [SCALARS, None, None],
    )


def relay(chain, value):
    def body(value_ref, out_ref):
        out_ref[...] = value_ref[...]

    return chain.run(body, [array(value.shape, value.dtype)], [value])[0]


def next_sum(chain, part, other):
    def body(part_ref, other_ref, send_ref, sum_ref):
        total = part_ref[...] + other_ref[...].astype(jnp.float32)
        sum_ref[...] = total
        send_ref[...] = total.astype(jnp.bfloat16)

    return chain.run(
        body, [array(part.shape, jnp.bfloat16), array(part.shape, jnp.float32)], [part, other]
    )


def middle_half(chain, places, mixed, residual_rows, gain):
    half, columns = mixed.shape

    def body(places_ref, mixed_ref, residual_ref, gain_ref, out_ref):
        span = pl.ds(pl.multiple_of(places_ref[1] * half, half), half)
        middle = residual_ref[span].astype(jnp.float32) + mixed_ref[...].astype(jnp.float32)
        out_ref[:, :columns] = (middle * gain_ref[...]).astype(jnp.bfloat16)
        out_ref[:, columns:] = jnp.broadcast_to(
            jnp.sum(middle * middle, axis=1, keepdims=True), (half, 128)
        ).astype(jnp.bfloat16)

    return chain.run(
        body,
        [array((half, columns + 128), jnp.bfloat16)],
        [places, mixed, residual_rows, gain],
        [SCALARS, None, None, None],
    )[0]


def middle_rows(chain, places, mixed, other, residual_rows, gain):
    half, columns = mixed.shape
    rows = 2 * half

    def body(places_ref, mixed_ref, other_ref, residual_ref, gain_ref, scaled_ref, middle_ref, squares_ref):
        for mine, ref in ((0, mixed_ref), (1, other_ref)):
            first = places_ref[1] if mine == 0 else 1 - places_ref[1]
            span = pl.ds(pl.multiple_of(first * half, half), half)
            middle = residual_ref[span].astype(jnp.float32) + ref[...].astype(jnp.float32)
            middle_ref[span] = middle
            scaled_ref[span] = (middle * gain_ref[...]).astype(jnp.bfloat16)
            squares_ref[span] = jnp.broadcast_to(
                jnp.sum(middle * middle, axis=1, keepdims=True), (half, 128)
            )

    return chain.run(
        body,
        [
            array((rows, columns), jnp.bfloat16),
            array((rows, columns), jnp.float32),
            array((rows, 128), jnp.float32),
        ],
        [places, mixed, other, residual_rows, gain],
        [SCALARS, None, None, None, None],
    )


def project(chain, scaled, squares, gate, up, start, width):
    half = scaled.shape[0] // 2

    def body(scaled_ref, gate_ref, up_ref, squares_ref, send_ref, keep_ref):
        for first, out_ref in ((half, send_ref), (0, keep_ref)):
            left = scaled_ref[first : first + half]
            for i, weight_ref in enumerate((gate_ref, up_ref)):
                out_ref[:, i * width : (i + 1) * width] = jnp.dot(
                    left, weight_ref[:, start : start + width], preferred_element_type=jnp.float32
                ).astype(jnp.bfloat16)

            out_ref[:, 2 * width :] = squares_ref[first : first + half].astype(jnp.bfloat16)

    out = array((half, 2 * width + 128), jnp.bfloat16)
    return chain.run(body, [out, out], [scaled, gate, up, squares])


def pair_order(size, pair):
    bits = size.bit_length() - 1
    sums = [bit for bit in range(bits) if bit != pair]
    spots = []
    for n in range(size):
        spot = (n & 1) << (bits - 1 - pair)
        for i, bit in enumerate(sums):
            spot |= ((n >> (bits - 1 - i)) & 1) << (bits - 1 - bit)
        spots.append(spot)
    return spots


def local_from_pair(size, pair):
    order = pair_order(size, pair)
    return [order.index(spot) for spot in range(size)]


def project_near(chain, places, scaled, gate, up, pair, area, start, skip, width, req_size):
    rows, depth = scaled.shape
    half, block = rows // 2, rows // req_size
    order = pair_order(req_size, pair)

    def body(places_ref, scaled_ref, gate_ref, up_ref, send_ref, keep_ref):
        mine = lax.rem(places_ref[0] // (1 << pair), 2)
        columns = pl.ds(pl.multiple_of(start + mine * area + skip, 128), width)
        for first, out_ref in ((req_size // 2, send_ref), (0, keep_ref)):
            left = jnp.concatenate(
                [
                    scaled_ref[spot * block : (spot + 1) * block]
                    for spot in order[first : first + req_size // 2]
                ],
                axis=0,
            )
            for i, weight_ref in enumerate((gate_ref, up_ref)):
                out_ref[:, i * width : (i + 1) * width] = jnp.dot(
                    left, weight_ref[:, columns], preferred_element_type=jnp.float32
                ).astype(jnp.bfloat16)

    out = array((half, 2 * width), jnp.bfloat16)
    return chain.run(body, [out, out], [places, scaled, gate, up], [SCALARS, None, None, None])


def project_pair(chain, places, near, squares, far, got, pair, skip, width, req_size):
    half = near[0].shape[0]
    rows = 2 * half
    block = rows // req_size
    depth = far[0].shape[1] - 128
    order = pair_order(req_size, pair)
    flip = 1 << (req_size.bit_length() - 2 - pair)
    cut = got[0].shape[0] - depth
    total = 2 * width + (0 if squares is None else 128)

    def body(places_ref, *refs):
        near_refs, (far_ref, away_ref), (early_ref, late_ref) = refs[:2], refs[2:4], refs[4:6]
        send_ref, keep_ref, all_far = refs[-3:]
        for away, ref in ((0, far_ref), (1, away_ref)):
            first = 1 - places_ref[1] if away else places_ref[1]
            all_far[pl.ds(pl.multiple_of(first * half, half), half)] = ref[...]
        outs = ((order[req_size // 2 :], send_ref), (order[: req_size // 2], keep_ref))

        def take(ref, spots, span, change=0):
            return jnp.concatenate(
                [
                    ref[(spot ^ change) * block : ((spot ^ change) + 1) * block, span]
                    for spot in spots
                ],
                axis=0,
            )

        for near_ref, (spots, out_ref) in zip(near_refs, outs, strict=True):
            for i in range(2):
                spans = [(early_ref, 0, 0, depth)]
                if i == 1:
                    spans = [(early_ref, depth, 0, cut), (late_ref, 0, cut, depth)]
                columns = slice(i * width, (i + 1) * width)
                product = near_ref[:, columns].astype(jnp.float32)
                for ref, top, begin, end in spans:
                    if end > begin:
                        product = product + jnp.dot(
                            take(all_far, spots, slice(begin, end), flip),
                            ref[top : top + end - begin, skip : skip + width],
                            preferred_element_type=jnp.float32,
                        )
                out_ref[:, columns] = product.astype(jnp.bfloat16)
            if squares is not None:
                out_ref[:, 2 * width :] = (
                    take(refs[6], spots, slice(0, 128))
                    + take(all_far, spots, slice(depth, depth + 128), flip).astype(jnp.float32)
                ).astype(jnp.bfloat16)

    ins = [places, *near, *far, *got] + ([] if squares is None else [squares])
    out = array((half, total), jnp.bfloat16)
    return chain.run(
        body,
        [out, out],
        ins,
        [SCALARS] + [None] * (len(ins) - 1),
        scratch=[pltpu.VMEM((rows, depth + 128), jnp.bfloat16)],
    )


def add_halve(chain, other, kept):
    half = kept.shape[0] // 2

    def body(other_ref, kept_ref, send_ref, keep_ref):
        for start, out_ref in ((half, send_ref), (0, keep_ref)):
            rows = slice(start, start + half)
            out_ref[...] = (
                other_ref[rows].astype(jnp.float32) + kept_ref[rows].astype(jnp.float32)
            ).astype(jnp.bfloat16)

    out = array((half, kept.shape[1]), jnp.bfloat16)
    return chain.run(body, [out, out], [other, kept])


def activate(chain, other, kept, inverse, width):
    rows = kept.shape[0]
    first = inverse is None

    def body(other_ref, kept_ref, *refs):
        def total(columns):
            return other_ref[:, columns].astype(jnp.float32) + kept_ref[:, columns].astype(
                jnp.float32
            )

        if first:
            hidden_ref, inverse_ref = refs
            scale = 1.0 / jnp.sqrt(total(slice(2 * width, 2 * width + 128)) / MODEL_WIDTH + EPS)
            inverse_ref[...] = scale
        else:
            scale_ref, hidden_ref = refs
            scale = scale_ref[:rows]
        scale = scale[:, :1]
        gate = total(slice(0, width)) * scale
        up = total(slice(width, 2 * width)) * scale
        hidden_ref[...] = (gate / (1.0 + jnp.exp(-gate)) * up).astype(jnp.bfloat16)

    outs = [array((rows, width), jnp.bfloat16)]
    ins = [other, kept]
    if first:
        outs.append(array((rows, 128), jnp.float32))
    else:
        ins.append(inverse)
    results = chain.run(body, outs, ins)
    return results if first else (results[0], inverse)


def join(chain, kept, other, after=()):
    rows = kept.shape[0]

    def body(kept_ref, other_ref, out_ref):
        out_ref[:rows] = kept_ref[...]
        out_ref[rows:] = other_ref[...]

    return chain.run(
        body, [array((2 * rows, kept.shape[1]), kept.dtype)], [kept, other], after=after
    )[0]


def lower(chain, places, kept, other, down, pair, area, start, skip, width, carried, req_size):
    columns = down.shape[1]
    paired = pair is not None
    rows = kept.shape[0] * (1 if paired else 2)
    half, block = rows // 2, rows // req_size
    back = local_from_pair(req_size, pair) if paired else None

    def body(places_ref, kept_ref, other_ref, down_ref, *refs):
        out_ref = refs[-1]

        def product(left, first):
            return jnp.dot(
                left, down_ref[pl.ds(first, width)], preferred_element_type=jnp.float32
            )

        def take(ref, flip):
            return jnp.concatenate(
                [ref[(n ^ flip) * block : ((n ^ flip) + 1) * block] for n in back], axis=0
            )

        if paired:
            mine = lax.rem(places_ref[0] // (1 << pair), 2)
            total = product(take(kept_ref, 0), pl.multiple_of(start + mine * area + skip, 128))
            total = total + product(
                take(other_ref, 1), pl.multiple_of(start + (1 - mine) * area + skip, 128)
            )
            out_ref[...] = total if carried is None else refs[0][...] + total
        else:
            for first, ref in ((0, kept_ref), (half, other_ref)):
                span = slice(first, first + half)
                total = product(ref[...], start)
                out_ref[span] = total if carried is None else refs[0][span] + total

    ins = [places, kept, other, down] + ([] if carried is None else [carried])
    return chain.run(
        body, [array((rows, columns), jnp.float32)], ins, [SCALARS] + [None] * (len(ins) - 1)
    )[0]


def split_for_kv(chain, total, places, req_size, kv_size):
    rows, columns = total.shape
    bits = req_size.bit_length() - 1
    block = rows // req_size
    per = req_size // kv_size

    def body(places_ref, total_ref, send_ref, keep_ref):
        req_place, mine = places_ref[0], places_ref[1]
        for spot in range(req_size):
            actual = req_place ^ bit_reverse(spot, bits)
            owner = actual // per
            start = pl.multiple_of(((owner // 2) * per + actual % per) * block, block)
            value = total_ref[spot * block : (spot + 1) * block].astype(jnp.bfloat16)

            @pl.when(owner % 2 == mine)
            def _():
                keep_ref[pl.ds(start, block)] = value

            @pl.when(owner % 2 != mine)
            def _():
                send_ref[pl.ds(start, block)] = value

    out = array((rows // 2, columns), jnp.bfloat16)
    return chain.run(
        body,
        [out, out],
        [places, total],
        [SCALARS, None],
    )


class Chunk:
    def __init__(self, pair, start, area, skip, width, bits):
        self.pair, self.start, self.area, self.skip, self.width = pair, start, area, skip, width
        self.sums = [bit for bit in range(bits) if bit != pair]
        self.gathers = [*reversed(self.sums), *([] if pair is None else [pair])]
        self.kept = self.moving = None


def areas_of(columns):
    tiles = columns // 128
    return tiles * 8 // 28 * 128, tiles * 6 // 28 * 128


def plan(columns, bits):
    first, second = areas_of(columns)
    rest = columns - 2 * first - 2 * second
    chunks = [Chunk(0, 0, first, 0, first, bits), Chunk(1, 2 * first, second, 0, second, bits)]
    if rest:
        chunks.insert(0, Chunk(None, columns - rest, 0, 0, rest, bits))
    stages = 2 * bits + 1
    tasks = [
        (i, stage)
        for stage in range(stages)
        for i, chunk in enumerate(chunks)
        if stage <= len(chunk.sums) + len(chunk.gathers)
    ]
    return chunks, tasks


def feed_forward(chain, places, scaled, squares, far_parts, gots, gate, up, down, req_size, kv_size):
    bits = req_size.bit_length() - 1
    total = None
    inverses = {}
    chunks, tasks = plan(gate.shape[1], bits)
    nears = [
        project_near(
            chain, places, scaled, gate, up, c.pair, c.area, c.start, c.skip, c.width, req_size
        )
        if c.pair is not None
        else None
        for c in chunks
    ]
    fars = [relay(chain, v) for v in far_parts]
    fars = [(v, kv_exchange(v, kv_size, 0)) for v in fars]
    for i, stage in tasks:
        chunk = chunks[i]
        pair, sums, gathers = chunk.pair, chunk.sums, chunk.gathers
        if stage == 0:
            if pair is not None:
                send, chunk.kept = project_pair(
                    chain,
                    places,
                    nears[i],
                    squares if chunk.skip == 0 else None,
                    fars[pair],
                    gots[pair],
                    pair,
                    chunk.skip,
                    chunk.width,
                    req_size,
                )
            else:
                send, chunk.kept = project(
                    chain, scaled, squares, gate, up, chunk.start, chunk.width
                )
            chunk.moving = exchange(send, req_size, sums[0])
        elif stage < len(sums):
            send, chunk.kept = add_halve(chain, chunk.moving, chunk.kept)
            chunk.moving = exchange(send, req_size, sums[stage])
        elif stage == len(sums):
            chunk.kept, inverses[pair] = activate(
                chain,
                chunk.moving,
                chunk.kept,
                inverses.get(pair),
                chunk.width,
            )
            chunk.moving = exchange(chunk.kept, req_size, gathers[0])
        elif stage < len(sums) + len(gathers):
            chunk.kept = join(chain, chunk.kept, chunk.moving)
            chunk.moving = exchange(chunk.kept, req_size, gathers[stage - len(sums)])
        else:
            total = lower(
                chain,
                places,
                chunk.kept,
                chunk.moving,
                down,
                pair,
                chunk.area,
                chunk.start,
                chunk.skip,
                chunk.width,
                total,
                req_size,
            )
    return total


def shards(
    residual_in,
    attn_gain,
    query_weight,
    key_matrix,
    value_matrix,
    key_cache,
    cached_values,
    cache_lengths,
    positions,
    output_weight,
    mlp_gain,
    gate_weight,
    up_weight,
    down_weight,
):
    req_size = lax.axis_size("req")
    kv_size = lax.axis_size("kv")
    req_place = lax.axis_index("req")
    kv_place = lax.axis_index("kv")
    local_rows = residual_in.shape[0] // req_size
    heads_here, head_size = key_cache.shape[1], key_cache.shape[3]
    tokens = lax.all_to_all(
        residual_in.reshape(req_size, local_rows, -1), "req", split_axis=0, concat_axis=0
    )
    features = query_weight.shape[1]
    places = jnp.stack([req_place, lax.rem(kv_place, 2), kv_place]).astype(jnp.int32)
    areas = areas_of(gate_weight.shape[1])
    theirs = []
    for pair, area in enumerate(areas):
        first = 2 * sum(areas[:pair]) + (1 - lax.rem(req_place // (1 << pair), 2)) * area
        slices = [lax.dynamic_slice_in_dim(v, first, area, 1) for v in (gate_weight, up_weight)]
        cut = EARLY_ROWS[pair] * gate_weight.shape[0] // 512
        early = jnp.concatenate([slices[0], slices[1][:cut]], axis=0) if cut else slices[0]
        theirs.append((early, slices[1][cut:]))
    start = corner(tokens)
    gots = [
        [exchange(tie(theirs[0][0], start, theirs[0][1], *theirs[1]), req_size, 0)],
        [exchange(tie(theirs[1][0], start), req_size, 1)],
    ]
    attended_rows = attention(
        tokens,
        attn_gain,
        (query_weight, key_matrix, value_matrix),
        (key_cache, cached_values),
        rotary_tables(positions, head_size),
        cache_lengths,
        heads_here,
        head_size,
    )
    chain = Chain(attended_rows)
    output_rows, residual_rows = fetch(
        chain, places, features, output_weight, residual_in, req_size
    )
    gathered = attended_rows
    bits = req_size.bit_length() - 1
    for bit in reversed(range(bits)):
        other = exchange(gathered, req_size, bit)
        early = {bits - 1: [gots[1][0]], 0: [gots[0][0]]}.get(bit, [])
        gathered = join(chain, gathered, other, early)
        if bit < 2:
            late = tie(theirs[bit][1], corner(gathered))
            gots[bit].append(exchange(late, req_size, bit))
    partial_mix = mix(chain, gathered, output_rows)
    gain = mlp_gain.reshape(1, -1)
    send, part = half_sum(chain, places, partial_mix, kv_exchange(partial_mix, kv_size, 0))
    for bit in range(1, kv_size.bit_length() - 1):
        send, part = next_sum(chain, part, kv_exchange(send, kv_size, bit))
    beside = kv_exchange(send, kv_size, 0)
    near_part = middle_half(chain, places, send, residual_rows, gain)
    far_parts = [exchange(near_part, req_size, pair) for pair in range(2)]
    scaled, middle, squares = middle_rows(chain, places, send, beside, residual_rows, gain)
    gate, up, down = gate_weight, up_weight, down_weight
    total = feed_forward(
        chain, places, scaled, squares, far_parts, gots, gate, up, down, req_size, kv_size
    )
    send, kept = split_for_kv(chain, total, places, req_size, kv_size)
    value = kept.astype(jnp.float32) + kv_exchange(send, kv_size, 0).astype(jnp.float32)
    for bit in reversed(range(1, kv_size.bit_length() - 1)):
        half = value.shape[0] // 2
        mine = lax.rem(kv_place >> bit, 2)
        other = kv_exchange(
            lax.dynamic_slice_in_dim(value, (1 - mine) * half, half, 0).astype(jnp.bfloat16),
            kv_size,
            bit,
        )
        value = lax.dynamic_slice_in_dim(value, mine * half, half, 0) + other.astype(jnp.float32)
    per = req_size // kv_size
    base_rows = jnp.concatenate(
        [
            lax.dynamic_slice_in_dim(
                middle,
                local_spot(req_place, kv_place * per + i, req_size) * local_rows,
                local_rows,
                0,
            )
            for i in range(per)
        ],
        axis=0,
    )
    return (base_rows + value).astype(jnp.bfloat16)


def solution(mesh):
    return jax.shard_map(
        shards,
        mesh=mesh,
        in_specs=(
            P(None, "req"),
            P(),
            P(None, "kv"),
            P(None, "kv"),
            P(None, "kv"),
            P("req", "kv", None, None),
            P("req", "kv", None, None),
            P("req"),
            P("req"),
            P(None, "req"),
            P("req"),
            P("req", "kv"),
            P("req", "kv"),
            P("kv", "req"),
        ),
        out_specs=P("kv", "req"),
        check_vma=False,
    )
```
